32 devices in a mesh: seq: 8 (over z, core), dp: 4 (over y, x).
Axes of the slice: x: 2, y: 2, z: 4, core: 2. Of those that a mesh axis runs over, the one named last changes fastest.
Arguments:
- tokens: bfloat16 [8, 512, 2048], P('dp', 'seq'), may hold values from -6 to 6
- segments: int32 [8, 512], P('dp'), may hold values from 0 to 7, as said below
- cotangent: bfloat16 [8, 512, 2048], P('dp', 'seq'), may hold values from -6 to 6
- attention_weight: float32 [2048, 4, 2048], P(('seq', 'dp'))
- attention_first: float32 [2048, 4, 2048], P(('seq', 'dp'))
- attention_second: float32 [2048, 4, 2048], P(('seq', 'dp'))
- feed_weight: float32 [2048, 3, 5120], P(('seq', 'dp'))
- feed_first: float32 [2048, 3, 5120], P(('seq', 'dp'))
- feed_second: float32 [2048, 3, 5120], P(('seq', 'dp'))
- gains: float32 [2, 2048], replicated, may hold values from 0.5 to 1.5
- gains_first: float32 [2, 2048], replicated, may hold values from -64 to 64
- gains_second: float32 [2, 2048], replicated, may hold values from 409.6 to 1638.4
- rel_table: float32 [32, 32], replicated, may hold values from -4 to 4
- table_first: float32 [32, 32], replicated, may hold values from -128 to 128
- table_second: float32 [32, 32], replicated, may hold values from 2048 to 8192
Outputs:
- block_out: bfloat16 [8, 512, 2048], P('dp', 'seq')
- grad_tokens: bfloat16 [8, 512, 2048], P('dp', 'seq')
- new_attention_weight: float32 [2048, 4, 2048], P(('seq', 'dp'))
- new_attention_first: float32 [2048, 4, 2048], P(('seq', 'dp'))
- new_attention_second: float32 [2048, 3, 2048], P(('seq', 'dp'))
- new_output_second: float32 [2048, 2048], P(('seq', 'dp'))
- new_feed_weight: float32 [2048, 3, 5120], P(('seq', 'dp'))
- new_feed_first: float32 [2048, 3, 5120], P(('seq', 'dp'))
- new_feed_second: float32 [2048, 3, 5120], P(('seq', 'dp'))
- new_gains: float32 [2, 2048], replicated
- new_gains_first: float32 [2, 2048], replicated
- new_gains_second: float32 [2, 2048], replicated
- new_table: float32 [32, 32], replicated
- new_table_first: float32 [32, 32], replicated
- new_table_second: float32 [32, 32], replicated
The draws below stay inside these ranges and needn't reach their ends.
Inputs may be any that keep to these rules, and one draw needn't show every extreme that they name: `segments`: along each row the numbers start at 0 and never fall, rising by at most one from a position to the next; tokens attend only within equal numbers. Of the 2 rows of each dp index, one holds a single document over all its positions, and every other row holds exactly 8 documents.
All inputs are finite; a program needn't handle non-finite values.
Results may differ from the reference program's by a relative error of at most 0.015.
The reference program's roundings to bfloat16 on the way count: a program that leaves them out, or rounds other values in their place, can miss the bound.
Values may be sent and summed in bfloat16 or wider, within the bound.
No kernel may reach another device: no remote copies, remote signals or barrier semaphores. Data moves between devices by JAX's collectives and lax.ppermute only.
A program may use at most 616 MiB of HBM per device.

```python
import math
import jax
import jax.numpy as jnp
from jax import lax

D = 2048
HEADS = 32
HEAD_DIM = 64
FF = 5120
NUM_BUCKETS = 32
MAX_DIST = 128
MICRO = 2
STEP = 10
SEQ_LEN = 512
ROWS = 8
TOKENS = 4096


def standard_noise(key, shape):
    return jnp.clip(jax.random.normal(key, shape, jnp.float32), -6.0, 6.0)


def second_noise(key, shape):
    return jnp.exp(jax.random.uniform(key, shape, jnp.float32, math.log(0.05), math.log(0.2)))


def attention_scales():
    return jnp.array([D ** (-0.5), (32 * D) ** (-0.5), D ** (-0.5), (HEADS * HEAD_DIM // 64) ** (-0.5)], jnp.float32)


def attention_grad_sq():
    return jnp.array([2.0, 50.0, 1.0, 0.015], jnp.float32) * TOKENS


def feed_scales():
    return jnp.array([D ** (-0.5), D ** (-0.5), FF ** (-0.5)], jnp.float32)


def feed_grad_sq():
    return jnp.array([0.15, 0.15, 0.42], jnp.float32) * TOKENS


def draw_attention_weight(key, part):
    noise = standard_noise(jax.random.fold_in(key, 11), (D, 4, HEADS * HEAD_DIM))
    return noise * attention_scales()[None, :, None]


def draw_attention_first(key, part):
    noise = standard_noise(jax.random.fold_in(key, 12), (D, 4, HEADS * HEAD_DIM))
    return noise * (0.111 * jnp.sqrt(attention_grad_sq()))[None, :, None]


def draw_attention_second(key, part):
    noise = second_noise(jax.random.fold_in(key, 13), (D, 4, HEADS * HEAD_DIM))
    return noise * attention_grad_sq()[None, :, None]


def draw_feed_weight(key, part):
    noise = standard_noise(jax.random.fold_in(key, 21), (D, 3, FF))
    return noise * feed_scales()[None, :, None]


def draw_feed_first(key, part):
    noise = standard_noise(jax.random.fold_in(key, 22), (D, 3, FF))
    return noise * (0.111 * jnp.sqrt(feed_grad_sq()))[None, :, None]


def draw_feed_second(key, part):
    noise = second_noise(jax.random.fold_in(key, 23), (D, 3, FF))
    return noise * feed_grad_sq()[None, :, None]


def draw_segments(key, part):
    start_key = jax.random.fold_in(key, 31)
    long_key = jax.random.fold_in(key, 32)
    break_count = 7
    row_keys = jax.random.split(start_key, ROWS)

    def row_breaks(row_key):
        return jax.random.permutation(row_key, SEQ_LEN - 1)[:break_count].astype(jnp.int32) + 1
    chosen = jax.vmap(row_breaks)(row_keys)
    position = jnp.arange(SEQ_LEN, dtype=jnp.int32)
    hits = jnp.sum((chosen[:, :, None] == position[None, None, :]).astype(jnp.int32), axis=1)
    single = (position[None, :] == 0).astype(jnp.int32)
    begins = hits + single
    long_pick = jax.random.randint(long_key, (ROWS // MICRO,), 0, MICRO)
    row_index = jnp.arange(ROWS, dtype=jnp.int32)
    is_long = row_index % MICRO == long_pick[row_index // MICRO]
    begins = jnp.where(is_long[:, None], single, begins)
    return (jnp.cumsum(begins, axis=1) - 1).astype(jnp.int32)


def shard_levels(stream_key, shape, cuts, least, high):
    def one(dim, parts):
        heights = jax.random.uniform(jax.random.fold_in(jax.random.fold_in(stream_key, 6), dim), (parts,), jnp.float32, least / len(cuts), high / len(cuts))
        return jnp.repeat(jnp.exp(heights), shape[dim] // parts).reshape((-1,) + (1,) * (len(shape) - dim - 1))

    loudness = one(*cuts[0])
    for cut in cuts[1:]:
        loudness = loudness * one(*cut)
    return loudness


def gaussian(stream_key, shape, deviation, reach, cuts=(), held_as=jnp.bfloat16):
    values = jax.random.normal(stream_key, shape, jnp.float32) * deviation
    if len(cuts) > 0:
        values = shard_levels(stream_key, shape, cuts, -0.22, 0.18) * values
    return jnp.clip(values, min=-reach, max=reach).astype(held_as)


def setup_inputs(seed: int = 0) -> dict:
    splits = jax.random.split(jax.random.key(seed), 16)
    return {
        "tokens": gaussian(splits[0], (ROWS, SEQ_LEN, D), 1.0, 6.0, ((0, 4), (1, 8))),
        "segments": draw_segments(jax.random.fold_in(splits[15], 71), 0),
        "cotangent": gaussian(splits[2], (ROWS, SEQ_LEN, D), 1.0, 6.0, ((0, 4), (1, 8))),
        "attention_weight": draw_attention_weight(jax.random.fold_in(splits[15], 71), 0),
        "attention_first": draw_attention_first(jax.random.fold_in(splits[15], 71), 0),
        "attention_second": draw_attention_second(jax.random.fold_in(splits[15], 71), 0),
        "feed_weight": draw_feed_weight(jax.random.fold_in(splits[15], 71), 0),
        "feed_first": draw_feed_first(jax.random.fold_in(splits[15], 71), 0),
        "feed_second": draw_feed_second(jax.random.fold_in(splits[15], 71), 0),
        "gains": jnp.clip(1.0 + 0.1 * jax.random.normal(splits[9], (2, D), jnp.float32), 0.5, 1.5),
        "gains_first": gaussian(splits[10], (2, D), (0.111 * (2 * TOKENS) ** 0.5), 64.0, (), jnp.float32),
        "gains_second": jnp.clip(jnp.exp(jax.random.uniform(splits[11], (2, D), jnp.float32, math.log(409.6), math.log(1638.4))), 409.6, 1638.4),
        "rel_table": gaussian(splits[12], (NUM_BUCKETS, HEADS), 1.0, 4.0, (), jnp.float32),
        "table_first": gaussian(splits[13], (NUM_BUCKETS, HEADS), (0.111 * (10 * TOKENS) ** 0.5), 128.0, (), jnp.float32),
        "table_second": jnp.clip(jnp.exp(jax.random.uniform(splits[14], (NUM_BUCKETS, HEADS), jnp.float32, math.log(2048.0), math.log(8192.0))), 2048.0, 8192.0),
    }


NORM_EPSILON = 1e-06
NEG_BIG = -1000000000.0
BETA_ONE = 0.9
BETA_TWO = 0.95
EPS_ADAM = 1e-08
DECAY = 0.1
HIGHEST = lax.Precision.HIGHEST

@jax.custom_vjp
def low(v):
    return lax.optimization_barrier(v.astype(jnp.bfloat16)).astype(jnp.float32)

@jax.custom_vjp
def low_back(v):
    return v

def low_keep(v):
    return (low(v), None)

def low_pass(kept, grad):
    return (grad,)

def back_keep(v):
    return (v, None)

def back_low(kept, grad):
    return (low(grad),)
low.defvjp(low_keep, low_pass)
low_back.defvjp(back_keep, back_low)

def rms_norm(values, gain_vec):
    inv_root = lax.rsqrt(lax.optimization_barrier(jnp.mean(values * values, axis=-1, keepdims=True)) + NORM_EPSILON)
    return values * inv_root * gain_vec

def gelu_tanh(values):
    return jax.nn.gelu(values, approximate=True)

def bucket_edges():
    half_count = NUM_BUCKETS // 2
    exact_count = half_count // 2
    log_count = half_count - exact_count
    far_ratio = MAX_DIST // exact_count
    edge_list = []
    for step_index in range(1, log_count):
        edge_at = exact_count
        while edge_at ** log_count < exact_count ** log_count * far_ratio ** step_index:
            edge_at = edge_at + 1
        edge_list.append(edge_at)
    return edge_list

def rel_bucket(relative):
    half_count = NUM_BUCKETS // 2
    exact_count = half_count // 2
    distance = jnp.abs(relative)
    far_bucket = jnp.full(relative.shape, exact_count, jnp.int32)
    for edge_at in bucket_edges():
        far_bucket = far_bucket + (distance >= edge_at).astype(jnp.int32)
    near_far = jnp.where(distance < exact_count, distance, far_bucket)
    return (near_far + jnp.where(relative > 0, half_count, 0)).astype(jnp.int32)

def matmul(left, right):
    return jnp.dot(left, right, precision=HIGHEST, preferred_element_type=jnp.float32)

def forward_row(inputs, seg_row, attention_weight, feed_weight, gains, rel_table):
    attention_low = low(attention_weight)
    feed_low = low(feed_weight)
    normed_one = low(rms_norm(inputs, gains[0]))
    queries = low_back(low(matmul(normed_one, attention_low[:, 0, :])))
    keys_all = low_back(low(matmul(normed_one, attention_low[:, 1, :])))
    values_all = low_back(low(matmul(normed_one, attention_low[:, 2, :])))
    query_heads = queries.reshape(SEQ_LEN, HEADS, HEAD_DIM)
    key_heads = keys_all.reshape(SEQ_LEN, HEADS, HEAD_DIM)
    value_heads = values_all.reshape(SEQ_LEN, HEADS, HEAD_DIM)
    positions = jnp.arange(SEQ_LEN, dtype=jnp.int32)
    block_rows = math.gcd(SEQ_LEN, 512)

    def attend_block(start):
        query_block = lax.dynamic_slice_in_dim(query_heads, start, block_rows, 0)
        seg_block = lax.dynamic_slice_in_dim(seg_row, start, block_rows, 0)
        query_location = start + jnp.arange(block_rows, dtype=jnp.int32)
        buckets = rel_bucket(positions[None, :] - query_location[:, None])
        biases = jnp.take(rel_table, buckets, axis=0).transpose(2, 0, 1)
        scores = jnp.einsum('qhd,khd->hqk', query_block, key_heads, precision=HIGHEST) + biases
        scores = low_back(scores)
        same_doc = (seg_block[:, None] == seg_row[None, :])[None]
        scores = jnp.where(same_doc, scores, NEG_BIG)
        row_max = lax.optimization_barrier(jnp.max(scores, axis=-1, keepdims=True))
        exp_scores = jnp.exp(scores - row_max)
        probs = low(exp_scores / lax.optimization_barrier(jnp.sum(exp_scores, axis=-1, keepdims=True)))
        return jnp.einsum('hqk,khd->qhd', probs, value_heads, precision=HIGHEST)
    starts = jnp.arange(0, SEQ_LEN, block_rows, dtype=jnp.int32)
    blocks = lax.map(jax.checkpoint(attend_block), starts)
    attended = low_back(low(blocks.reshape(SEQ_LEN, HEADS * HEAD_DIM)))
    attention_out = low_back(matmul(attended, attention_low[:, 3, :].T))
    hidden_state = inputs + attention_out
    normed_two = low(rms_norm(hidden_state, gains[1]))
    gate_pre = low_back(matmul(normed_two, feed_low[:, 0, :]))
    up_pre = low_back(matmul(normed_two, feed_low[:, 1, :]))
    inner = low(gelu_tanh(gate_pre) * up_pre)
    feed_out = low_back(matmul(inner, feed_low[:, 2, :].T))
    return hidden_state + feed_out

def adam_update(weight, first, second, grads, rate, decay):
    first_new = BETA_ONE * first + (1.0 - BETA_ONE) * grads
    second_new = BETA_TWO * second + (1.0 - BETA_TWO) * grads * grads
    first_hat = first_new / (1.0 - BETA_ONE ** STEP)
    second_hat = second_new / (1.0 - BETA_TWO ** STEP)
    weight_new = weight - rate * (first_hat / (jnp.sqrt(second_hat) + EPS_ADAM) + decay * weight)
    return (weight_new, first_new, second_new)

def attention_rates():
    return 3.0 * jnp.array([D ** (-0.5), (32 * D) ** (-0.5), D ** (-0.5), (HEADS * HEAD_DIM // 64) ** (-0.5)], jnp.float32).reshape(1, 4, 1)

def feed_rates():
    return 3.0 * jnp.array([D ** (-0.5), D ** (-0.5), FF ** (-0.5)], jnp.float32).reshape(1, 3, 1)

def reference(tokens, segments, cotangent, attention_weight, attention_first, attention_second, feed_weight, feed_first, feed_second, gains, gains_first, gains_second, rel_table, table_first, table_second):

    def row_step(totals, row_contents):
        inputs, seg_row, grad_out = row_contents

        def forward_here(input_rows, attention_w, feed_w, gain_w, table_w):
            return forward_row(input_rows, seg_row, attention_w, feed_w, gain_w, table_w)
        out_row, back_fn = jax.vjp(forward_here, inputs.astype(jnp.float32), attention_weight, feed_weight, gains, rel_table)
        grads = back_fn(grad_out.astype(jnp.float32))
        new_totals = tuple((total + grad for total, grad in zip(totals, grads[1:])))
        return (new_totals, (out_row.astype(jnp.bfloat16), grads[0].astype(jnp.bfloat16)))
    init = (jnp.zeros(attention_weight.shape, jnp.float32), jnp.zeros(feed_weight.shape, jnp.float32), jnp.zeros(gains.shape, jnp.float32), jnp.zeros(rel_table.shape, jnp.float32))
    totals, outs = lax.scan(row_step, init, (tokens, segments, cotangent))
    block_out, grad_tokens = outs
    grad_attention, grad_feed, grad_gains, grad_table = totals
    new_attention = adam_update(attention_weight, attention_first, attention_second, grad_attention, attention_rates(), DECAY)
    new_feed = adam_update(feed_weight, feed_first, feed_second, grad_feed, feed_rates(), DECAY)
    new_gains = adam_update(gains, gains_first, gains_second, grad_gains, 0.6, 0.0)
    new_table = adam_update(rel_table, table_first, table_second, grad_table, 1.5, 0.0)
    return (block_out, grad_tokens, new_attention[0], new_attention[1], new_attention[2][:, :3, :], new_attention[2][:, 3, :], new_feed[0], new_feed[1], new_feed[2], new_gains[0], new_gains[1], new_gains[2], new_table[0], new_table[1], new_table[2])
```

```python
import jax
import jax.numpy as jnp
from jax import lax
from jax.sharding import PartitionSpec as P

D = 2048
HEADS = 32
HEAD_DIM = 64
FF = 5120
NUM_BUCKETS = 32
MAX_DIST = 128
STEP = 10


NORM_EPSILON = 1e-06
NEG_BIG = -1000000000.0
BETA_ONE = 0.9
BETA_TWO = 0.95
EPS_ADAM = 1e-08
DECAY = 0.1
HIGHEST = lax.Precision.HIGHEST


def rms_norm(values, gain_vec):
    inv_root = lax.rsqrt(jnp.mean(values * values, axis=-1, keepdims=True) + NORM_EPSILON)
    return values * inv_root * gain_vec


def gelu_tanh(values):
    return jax.nn.gelu(values, approximate=True)


def bucket_edges():
    half_count = NUM_BUCKETS // 2
    exact_count = half_count // 2
    log_count = half_count - exact_count
    far_ratio = MAX_DIST // exact_count
    edge_list = []
    for step_index in range(1, log_count):
        edge_at = exact_count
        while edge_at**log_count < exact_count**log_count * far_ratio**step_index:
            edge_at = edge_at + 1
        edge_list.append(edge_at)
    return edge_list


def rel_bucket(relative):
    half_count = NUM_BUCKETS // 2
    exact_count = half_count // 2
    distance = jnp.abs(relative)
    far_bucket = jnp.full(relative.shape, exact_count, jnp.int32)
    for edge_at in bucket_edges():
        far_bucket = far_bucket + (distance >= edge_at).astype(jnp.int32)
    near_far = jnp.where(distance < exact_count, distance, far_bucket)
    return near_far + jnp.where(relative > 0, half_count, 0)


def adam_update(weight, first, second, grads, rate, decay):
    first_new = BETA_ONE * first + (1.0 - BETA_ONE) * grads
    second_new = BETA_TWO * second + (1.0 - BETA_TWO) * grads * grads
    first_hat = first_new / (1.0 - BETA_ONE**STEP)
    second_hat = second_new / (1.0 - BETA_TWO**STEP)
    weight_new = weight - rate * (first_hat / (jnp.sqrt(second_hat) + EPS_ADAM) + decay * weight)
    return (weight_new, first_new, second_new)


def attention_rates():
    return 3.0 * jnp.array(
        [D ** (-0.5), (32 * D) ** (-0.5), D ** (-0.5), (HEADS * HEAD_DIM // 64) ** (-0.5)],
        jnp.float32,
    ).reshape(1, 4, 1)


def feed_rates():
    return 3.0 * jnp.array([D ** (-0.5), D ** (-0.5), FF ** (-0.5)], jnp.float32).reshape(1, 3, 1)


def dot(left, right):
    return jnp.dot(left, right, preferred_element_type=jnp.float32)


def dot_t(left, right):
    return lax.dot_general(
        left, right, (((1,), (1,)), ((), ())), preferred_element_type=jnp.float32
    )


def outer_sum(left, right):
    return lax.dot_general(
        left, right, (((0,), (0,)), ((), ())), preferred_element_type=jnp.float32
    )


def norm_stats(values):
    return lax.rsqrt(jnp.mean(values * values, axis=-1, keepdims=True) + NORM_EPSILON)


def norm_back(values, gain_vec, grads):
    inv_root = norm_stats(values)
    unit = values * inv_root
    scaled = grads * gain_vec
    grad_in = inv_root * (scaled - unit * jnp.mean(unit * scaled, axis=-1, keepdims=True))
    return grad_in, jnp.sum(grads * unit, axis=(0, 1))


def to_columns(weight):
    seq_size = lax.axis_size("seq")
    dp_size = lax.axis_size("dp")
    rows, slots, width = weight.shape
    part = width // seq_size
    send = weight.astype(jnp.bfloat16).reshape(rows, slots, seq_size, part).transpose(2, 0, 1, 3)
    send = send.reshape(seq_size, rows, slots * part)
    mine = lax.all_to_all(send, "seq", 0, 0)
    full = lax.all_gather(mine, "dp", axis=0)
    return full.transpose(1, 0, 2, 3).reshape(seq_size * dp_size * rows, slots * part)


def to_rows(grad, slots):
    seq_size = lax.axis_size("seq")
    dp_size = lax.axis_size("dp")
    rows = grad.shape[0] // (seq_size * dp_size)
    part = grad.shape[1] // slots
    send = grad.astype(jnp.bfloat16).reshape(seq_size, dp_size, rows, slots * part).transpose(1, 0, 2, 3)
    summed = lax.psum_scatter(send, "dp", scatter_dimension=0)
    back = lax.all_to_all(summed, "seq", 0, 0)
    back = back.reshape(seq_size, rows, slots, part).transpose(1, 2, 0, 3)
    return back.reshape(rows, slots, seq_size * part).astype(jnp.float32)


def gather_tokens(local_rows):
    full = lax.all_gather(local_rows, "seq", axis=0)
    return full.reshape(-1, local_rows.shape[-1])


def scatter_tokens(partial, shape):
    send = partial.astype(jnp.bfloat16).reshape((lax.axis_size("seq"),) + shape)
    return lax.psum_scatter(send, "seq", scatter_dimension=0).astype(jnp.float32)


def local(
    tokens,
    segments,
    cotangent,
    attention_weight,
    attention_first,
    attention_second,
    feed_weight,
    feed_first,
    feed_second,
    gains,
    gains_first,
    gains_second,
    rel_table,
    table_first,
    table_second,
):
    micro_count, local_rows, width = tokens.shape
    shape = tokens.shape
    seq_size = lax.axis_size("seq")
    seq_len = local_rows * seq_size
    heads_here = HEADS // seq_size
    part = heads_here * HEAD_DIM
    hidden_part = FF // seq_size
    seq_index = lax.axis_index("seq")

    attention_low = to_columns(attention_weight)
    feed_low = to_columns(feed_weight)
    weight_qkv = attention_low[:, : 3 * part]
    weight_out = attention_low[:, 3 * part :]
    weight_in = feed_low[:, : 2 * hidden_part]
    weight_down = feed_low[:, 2 * hidden_part :]

    positions = jnp.arange(seq_len, dtype=jnp.int32)
    buckets = rel_bucket(positions[None, :] - positions[:, None])
    bucket_match = buckets[None, :, :] == jnp.arange(NUM_BUCKETS, dtype=jnp.int32)[:, None, None]
    table_here = lax.dynamic_slice_in_dim(rel_table, seq_index * heads_here, heads_here, 1)
    bias = jnp.einsum(
        "atj,ao->otj",
        bucket_match.astype(jnp.float32),
        table_here,
        precision=HIGHEST,
        preferred_element_type=jnp.float32,
    )
    same_doc = segments[:, :, None] == segments[:, None, :]

    def to_heads(matrix):
        grouped = matrix.reshape(seq_size, micro_count, local_rows, heads_here, HEAD_DIM)
        return grouped.transpose(1, 3, 0, 2, 4).reshape(micro_count, heads_here, seq_len, HEAD_DIM)

    def from_heads(grouped):
        split = grouped.reshape(micro_count, heads_here, seq_size, local_rows, HEAD_DIM)
        return split.transpose(2, 0, 3, 1, 4).reshape(seq_len * micro_count, part)

    inputs = tokens.astype(jnp.float32)
    normed_one = gather_tokens(rms_norm(inputs, gains[0]).astype(jnp.bfloat16))
    grad_out = gather_tokens(cotangent)
    qkv = dot(normed_one, weight_qkv).astype(jnp.bfloat16)
    query_h = to_heads(qkv[:, :part])
    key_h = to_heads(qkv[:, part : 2 * part])
    value_h = to_heads(qkv[:, 2 * part :])
    scores = jnp.einsum("bhqd,bhkd->bhqk", query_h, key_h, preferred_element_type=jnp.float32)
    scores = jnp.where(same_doc[:, None], scores + bias[None], NEG_BIG)
    row_max = jnp.max(scores, axis=-1, keepdims=True)
    exp_scores = jnp.exp(scores - row_max)
    probs = exp_scores / jnp.sum(exp_scores, axis=-1, keepdims=True)
    probs_low = probs.astype(jnp.bfloat16)
    attended = from_heads(
        jnp.einsum("bhqk,bhkd->bhqd", probs_low, value_h, preferred_element_type=jnp.float32)
    ).astype(jnp.bfloat16)
    hidden_state = inputs + scatter_tokens(dot_t(attended, weight_out), shape)
    normed_two = gather_tokens(rms_norm(hidden_state, gains[1]).astype(jnp.bfloat16))
    pre = dot(normed_two, weight_in)
    gate_pre = pre[:, :hidden_part]
    up_pre = pre[:, hidden_part:]
    gate_act, gate_back = jax.vjp(gelu_tanh, gate_pre)
    inner = (gate_act * up_pre).astype(jnp.bfloat16)
    block_rows = (hidden_state + scatter_tokens(dot_t(inner, weight_down), shape)).astype(jnp.bfloat16)
    grad_inner = dot(grad_out, weight_down)
    grad_gate = gate_back(grad_inner * up_pre)[0].astype(jnp.bfloat16)
    grad_up = (grad_inner * gate_act).astype(jnp.bfloat16)
    grad_pre = jnp.concatenate([grad_gate, grad_up], 1)
    grad_normed_two = scatter_tokens(dot_t(grad_pre, weight_in), shape)
    grad_feed = jnp.concatenate([outer_sum(normed_two, grad_pre), outer_sum(grad_out, inner)], 1)
    feed_total = to_rows(grad_feed, 3)
    grad_hidden_norm, grad_gain_two = norm_back(hidden_state, gains[1], grad_normed_two)
    grad_hidden = cotangent.astype(jnp.float32) + grad_hidden_norm
    grad_branch = gather_tokens(grad_hidden.astype(jnp.bfloat16))
    grad_attended = to_heads(dot(grad_branch, weight_out).astype(jnp.bfloat16))
    grad_probs = jnp.einsum(
        "bhqd,bhkd->bhqk", grad_attended, value_h, preferred_element_type=jnp.float32
    )
    row_dot = jnp.sum(probs * grad_probs, axis=-1, keepdims=True)
    grad_scores = (probs * (grad_probs - row_dot)).astype(jnp.bfloat16)
    grad_query = jnp.einsum("bhqk,bhkd->bhqd", grad_scores, key_h, preferred_element_type=jnp.float32)
    grad_key = jnp.einsum("bhqk,bhqd->bhkd", grad_scores, query_h, preferred_element_type=jnp.float32)
    grad_value = jnp.einsum(
        "bhqk,bhqd->bhkd", probs_low, grad_attended, preferred_element_type=jnp.float32
    )
    grad_table_here = jnp.einsum(
        "bhij,zij->zh",
        grad_scores,
        bucket_match.astype(jnp.bfloat16),
        preferred_element_type=jnp.float32,
    )
    grad_qkv = jnp.concatenate(
        [from_heads(item.astype(jnp.bfloat16)) for item in (grad_query, grad_key, grad_value)], 1
    )
    grad_normed_one = scatter_tokens(dot_t(grad_qkv, weight_qkv), shape)
    grad_attention = jnp.concatenate(
        [outer_sum(normed_one, grad_qkv), outer_sum(grad_branch, attended)], 1
    )
    attention_total = to_rows(grad_attention, 4)
    grad_input_norm, grad_gain_one = norm_back(inputs, gains[0], grad_normed_one)
    grad_rows = (grad_hidden + grad_input_norm).astype(jnp.bfloat16)
    grad_table = lax.dynamic_update_slice_in_dim(
        jnp.zeros((NUM_BUCKETS, HEADS), jnp.float32), grad_table_here, seq_index * heads_here, 1
    )
    gains_total, table_total = lax.psum(
        (jnp.stack([grad_gain_one, grad_gain_two], 0), grad_table), ("seq", "dp")
    )
    new_attention = adam_update(
        attention_weight,
        attention_first,
        attention_second,
        attention_total,
        attention_rates(),
        DECAY,
    )
    new_feed = adam_update(feed_weight, feed_first, feed_second, feed_total, feed_rates(), DECAY)
    new_gains = adam_update(gains, gains_first, gains_second, gains_total, 0.6, 0.0)
    new_table = adam_update(rel_table, table_first, table_second, table_total, 1.5, 0.0)
    return (
        block_rows,
        grad_rows,
        new_attention[0],
        new_attention[1],
        new_attention[2][:, :3, :],
        new_attention[2][:, 3, :],
        new_feed[0],
        new_feed[1],
        new_feed[2],
        new_gains[0],
        new_gains[1],
        new_gains[2],
        new_table[0],
        new_table[1],
        new_table[2],
    )


def solution(mesh):
    in_specs = (
        P("dp", "seq", None),
        P("dp", None),
        P("dp", "seq", None),
        P(("seq", "dp"), None, None),
        P(("seq", "dp"), None, None),
        P(("seq", "dp"), None, None),
        P(("seq", "dp"), None, None),
        P(("seq", "dp"), None, None),
        P(("seq", "dp"), None, None),
        P(),
        P(),
        P(),
        P(),
        P(),
        P(),
    )
    out_specs = (
        P("dp", "seq", None),
        P("dp", "seq", None),
        P(("seq", "dp"), None, None),
        P(("seq", "dp"), None, None),
        P(("seq", "dp"), None, None),
        P(("seq", "dp"), None),
        P(("seq", "dp"), None, None),
        P(("seq", "dp"), None, None),
        P(("seq", "dp"), None, None),
        P(),
        P(),
        P(),
        P(),
        P(),
        P(),
    )
    return jax.shard_map(local, mesh=mesh, in_specs=in_specs, out_specs=out_specs, check_vma=False)
```

```python
import jax
import jax.numpy as jnp
from jax import lax
from jax.experimental import pallas as pl
from jax.experimental.pallas import tpu as pltpu
from jax.sharding import PartitionSpec as P

D = 2048
HEADS = 32
HEAD_DIM = 64
FF = 5120
NUM_BUCKETS = 32
MAX_DIST = 128
STEP = 10


NORM_EPSILON = 1e-06
NEG_BIG = -1000000000.0
BETA_ONE = 0.9
BETA_TWO = 0.95
EPS_ADAM = 1e-08
DECAY = 0.1
HIGHEST = lax.Precision.HIGHEST


def rms_norm(values, gain_vec):
    inv_root = lax.rsqrt(jnp.mean(values * values, axis=-1, keepdims=True) + NORM_EPSILON)
    return values * inv_root * gain_vec


def gelu_tanh(values):
    return jax.nn.gelu(values, approximate=True)


def bucket_edges():
    half_count = NUM_BUCKETS // 2
    exact_count = half_count // 2
    log_count = half_count - exact_count
    far_ratio = MAX_DIST // exact_count
    edge_list = []
    for step_index in range(1, log_count):
        edge_at = exact_count
        while edge_at**log_count < exact_count**log_count * far_ratio**step_index:
            edge_at = edge_at + 1
        edge_list.append(edge_at)
    return edge_list


def rel_bucket(relative):
    half_count = NUM_BUCKETS // 2
    exact_count = half_count // 2
    distance = jnp.abs(relative)
    far_bucket = jnp.full(relative.shape, exact_count, jnp.int32)
    for edge_at in bucket_edges():
        far_bucket = far_bucket + (distance >= edge_at).astype(jnp.int32)
    near_far = jnp.where(distance < exact_count, distance, far_bucket)
    return near_far + jnp.where(relative > 0, half_count, 0)


def adam_update(weight, first, second, grads, rate, decay):
    first_new = BETA_ONE * first + (1.0 - BETA_ONE) * grads
    second_new = BETA_TWO * second + (1.0 - BETA_TWO) * grads * grads
    first_hat = first_new / (1.0 - BETA_ONE**STEP)
    second_hat = second_new / (1.0 - BETA_TWO**STEP)
    weight_new = weight - rate * (first_hat / (jnp.sqrt(second_hat) + EPS_ADAM) + decay * weight)
    return (weight_new, first_new, second_new)


def attention_rates():
    return 3.0 * jnp.array(
        [D ** (-0.5), (32 * D) ** (-0.5), D ** (-0.5), (HEADS * HEAD_DIM // 64) ** (-0.5)],
        jnp.float32,
    ).reshape(1, 4, 1)


def feed_rates():
    return 3.0 * jnp.array([D ** (-0.5), D ** (-0.5), FF ** (-0.5)], jnp.float32).reshape(1, 3, 1)


def dot(left, right):
    return jnp.dot(left, right, preferred_element_type=jnp.float32)


def dot_t(left, right):
    return lax.dot_general(
        left, right, (((1,), (1,)), ((), ())), preferred_element_type=jnp.float32
    )


def outer_sum(left, right):
    return lax.dot_general(
        left, right, (((0,), (0,)), ((), ())), preferred_element_type=jnp.float32
    )


def norm_stats(values):
    return lax.rsqrt(jnp.mean(values * values, axis=-1, keepdims=True) + NORM_EPSILON)


def norm_back(values, gain_vec, grads):
    inv_root = norm_stats(values)
    unit = values * inv_root
    scaled = grads * gain_vec
    grad_in = inv_root * (scaled - unit * jnp.mean(unit * scaled, axis=-1, keepdims=True))
    return grad_in, jnp.sum(grads * unit, axis=(0, 1))


def partner_pairs(axis, offset):
    return [(index, index ^ offset) for index in range(lax.axis_size(axis))]


def swap(value, axis, offset):
    return lax.ppermute(value, axis, partner_pairs(axis, offset))


VMEM_LIMIT = 56 * 1024 * 1024


def place_columns(stacked, me):
    seq_size, slots, rows, part = stacked.shape
    if part % 128:
        out = jnp.zeros((slots, rows, seq_size * part), stacked.dtype)
        for offset in range(seq_size):
            out = lax.dynamic_update_slice(out, stacked[offset], (0, 0, (me ^ offset) * part))
        return out

    def body(me_ref, in_ref, out_ref):
        out_ref[...] = in_ref[0]

    return pl.pallas_call(
        body,
        grid_spec=pltpu.PrefetchScalarGridSpec(
            num_scalar_prefetch=1,
            grid=(seq_size,),
            in_specs=[
                pl.BlockSpec((1, slots, rows, part), lambda j, me_ref: (j ^ me_ref[0], 0, 0, 0))
            ],
            out_specs=pl.BlockSpec((slots, rows, part), lambda j, me_ref: (0, 0, j)),
        ),
        out_shape=jax.ShapeDtypeStruct((slots, rows, seq_size * part), stacked.dtype),
        compiler_params=pltpu.CompilerParams(vmem_limit_bytes=VMEM_LIMIT),
    )(me.reshape(1), stacked)


def head_probs(query, key, bias, same_doc):
    scores = lax.dot_general(
        query, key, (((1,), (1,)), ((), ())), preferred_element_type=jnp.float32
    )
    scores = jnp.where(same_doc, scores + bias, NEG_BIG)
    exp_scores = jnp.exp(scores - jnp.max(scores, axis=-1, keepdims=True))
    return exp_scores * (1.0 / jnp.sum(exp_scores, axis=-1, keepdims=True))


def attention_specs(seq_size, rows):
    length = seq_size * rows
    tokens_spec = pl.BlockSpec((seq_size, 1, rows, 128), lambda pair, m: (0, m, 0, pair))
    return tokens_spec, [
        pl.BlockSpec((2, length, length), lambda pair, m: (pair, 0, 0)),
        pl.BlockSpec((1, length, 1), lambda pair, m: (m, 0, 0)),
        pl.BlockSpec((1, 1, length), lambda pair, m: (m, 0, 0)),
    ]


def attention_forward(query, key, value, bias, segments):
    seq_size, micro_count, rows, part = query.shape
    length = seq_size * rows
    tokens_spec, other_specs = attention_specs(seq_size, rows)

    def body(q_ref, k_ref, v_ref, bias_ref, seg_q_ref, seg_k_ref, out_ref):
        q, k, v = [ref[:, 0].reshape(length, 128) for ref in (q_ref, k_ref, v_ref)]
        same_doc = seg_q_ref[0] == seg_k_ref[0]
        outs = []
        for h in range(2):
            cols = slice(h * HEAD_DIM, (h + 1) * HEAD_DIM)
            probs = head_probs(q[:, cols], k[:, cols], bias_ref[h], same_doc)
            outs.append(dot(probs.astype(jnp.bfloat16), v[:, cols]))
        out = jnp.concatenate(outs, 1).astype(jnp.bfloat16)
        out_ref[...] = out.reshape(seq_size, 1, rows, 128)

    return pl.pallas_call(
        body,
        grid=(part // 128, micro_count),
        in_specs=[tokens_spec] * 3 + other_specs,
        out_specs=tokens_spec,
        out_shape=jax.ShapeDtypeStruct(query.shape, jnp.bfloat16),
        compiler_params=pltpu.CompilerParams(vmem_limit_bytes=VMEM_LIMIT),
    )(query, key, value, bias, segments[:, :, None], segments[:, None, :])


def attention_backward(query, key, value, grad_out, bias, segments):
    seq_size, micro_count, rows, part = query.shape
    length = seq_size * rows
    tokens_spec, other_specs = attention_specs(seq_size, rows)

    def body(
        q_ref, k_ref, v_ref, g_ref, bias_ref, seg_q_ref, seg_k_ref, dq_ref, dk_ref, dv_ref, ds_ref
    ):
        q, k, v, g = [ref[:, 0].reshape(length, 128) for ref in (q_ref, k_ref, v_ref, g_ref)]
        same_doc = seg_q_ref[0] == seg_k_ref[0]
        first = pl.program_id(1) == 0
        grads = ([], [], [])
        for h in range(2):
            cols = slice(h * HEAD_DIM, (h + 1) * HEAD_DIM)
            probs = head_probs(q[:, cols], k[:, cols], bias_ref[h], same_doc)
            grad_probs = dot_t(g[:, cols], v[:, cols])
            row_dot = jnp.sum(probs * grad_probs, axis=-1, keepdims=True)
            grad_scores = (probs * (grad_probs - row_dot)).astype(jnp.bfloat16)
            wide = grad_scores.astype(jnp.float32)
            ds_ref[h] = jnp.where(first, wide, ds_ref[h] + wide)
            grads[0].append(dot(grad_scores, k[:, cols]))
            grads[1].append(outer_sum(grad_scores, q[:, cols]))
            grads[2].append(outer_sum(probs.astype(jnp.bfloat16), g[:, cols]))
        for ref, parts in zip((dq_ref, dk_ref, dv_ref), grads):
            joined = jnp.concatenate(parts, 1).astype(jnp.bfloat16)
            ref[...] = joined.reshape(seq_size, 1, rows, 128)

    return pl.pallas_call(
        body,
        grid=(part // 128, micro_count),
        in_specs=[tokens_spec] * 4 + other_specs,
        out_specs=[tokens_spec] * 3
        + [pl.BlockSpec((2, length, length), lambda pair, m: (pair, 0, 0))],
        out_shape=[jax.ShapeDtypeStruct(query.shape, jnp.bfloat16)] * 3
        + [jax.ShapeDtypeStruct((part // HEAD_DIM, length, length), jnp.float32)],
        compiler_params=pltpu.CompilerParams(vmem_limit_bytes=VMEM_LIMIT),
    )(query, key, value, grad_out, bias, segments[:, :, None], segments[:, None, :])


def exchange(values, dim, out_dim):
    seq_size = lax.axis_size("seq")
    me = lax.axis_index("seq")
    received = None
    for offset in range(seq_size):
        piece = lax.dynamic_index_in_dim(values, me ^ offset, dim, keepdims=False)
        if offset:
            piece = swap(piece, "seq", offset)
        piece = jnp.expand_dims(piece, out_dim)
        if received is None:
            shape = piece.shape[:out_dim] + (seq_size,) + piece.shape[out_dim + 1 :]
            received = jnp.zeros(shape, values.dtype)
        received = lax.dynamic_update_slice_in_dim(received, piece, me ^ offset, out_dim)
    return received


def gather_dp(mine):
    if lax.axis_size("dp") != 4:
        return lax.all_gather(mine, "dp", axis=2)
    me = lax.axis_index("dp")
    half = mine.shape[1] // 2
    one = swap(mine, "dp", 1)
    two = swap(mine, "dp", 2)
    low = swap(one[:, :half], "dp", 2)
    high = swap(two[:, half:], "dp", 1)
    full = jnp.zeros(mine.shape[:2] + (4,) + mine.shape[2:], mine.dtype)
    for piece, source, start in (
        (mine, 0, 0),
        (one, 1, 0),
        (two, 2, 0),
        (low, 3, 0),
        (high, 3, half),
    ):
        full = lax.dynamic_update_slice(full, piece[:, :, None], (0, start, me ^ source, 0, 0))
    return full


def wide(value):
    return value.astype(jnp.float32)


def scatter_dp_first(partial):
    if lax.axis_size("dp") != 4:
        return [lax.psum_scatter(partial, "dp", scatter_dimension=2)]
    me = lax.axis_index("dp")
    half = partial.shape[1] // 2
    pieces = [lax.dynamic_index_in_dim(partial, me ^ k, 2, keepdims=False) for k in range(4)]
    low = [piece[:, :half] for piece in pieces]
    high = [piece[:, half:] for piece in pieces]
    low_two = (wide(low[2]) + wide(swap(low[3], "dp", 1))).astype(jnp.bfloat16)
    high_one = (wide(high[1]) + wide(swap(high[3], "dp", 2))).astype(jnp.bfloat16)
    low_zero = wide(low[0]) + wide(swap(low[1], "dp", 1))
    high_zero = wide(high[0]) + wide(swap(high[2], "dp", 2))
    return [low_two, high_one, low_zero, high_zero]


def scatter_dp_second(items):
    if len(items) == 1:
        return items[0]
    low_two, high_one, low_zero, high_zero = items
    low_sum = low_zero + wide(swap(low_two, "dp", 2))
    high_sum = high_zero + wide(swap(high_one, "dp", 1))
    return jnp.concatenate([low_sum, high_sum], 1).astype(jnp.bfloat16)


def to_columns(weight):
    seq_size = lax.axis_size("seq")
    slots, rows, width = weight.shape
    part = width // seq_size
    return exchange(weight.astype(jnp.bfloat16).reshape(slots, rows, seq_size, part), 2, 1)


def all_rows(mine):
    return gather_dp(mine).reshape(mine.shape[0], -1, mine.shape[-1])


def after(value, *earlier):
    return lax.optimization_barrier((value,) + earlier)[0]


def to_rows_first(grads):
    seq_size = lax.axis_size("seq")
    dp_size = lax.axis_size("dp")
    partial = jnp.stack([grad.astype(jnp.bfloat16) for grad in grads], 0)
    slots, total, part = partial.shape
    rows = total // (seq_size * dp_size)
    return scatter_dp_first(partial.reshape(slots, seq_size, dp_size, rows, part))


def to_rows_last(mine):
    me = lax.axis_index("seq")
    pieces = []
    for offset in range(lax.axis_size("seq")):
        piece = lax.dynamic_index_in_dim(mine, me ^ offset, 1, keepdims=False)
        pieces.append(swap(piece, "seq", offset) if offset else piece)
    return wide(place_columns(jnp.stack(pieces, 0), me))


def sum_all(value):
    for axis in ("seq", "dp"):
        offset = 1
        while offset < lax.axis_size(axis):
            value = value + swap(value, axis, offset)
            offset = offset * 2
    return value


def gather_tokens(local_rows):
    full = lax.all_gather(local_rows, "seq", axis=0)
    return full.reshape(-1, local_rows.shape[-1])


def scatter_tokens(partial, shape):
    send = partial.astype(jnp.bfloat16).reshape((lax.axis_size("seq"),) + shape)
    return lax.psum_scatter(send, "seq", scatter_dimension=0).astype(jnp.float32)


def local(
    tokens,
    segments,
    cotangent,
    attention_weight,
    attention_first,
    attention_second,
    feed_weight,
    feed_first,
    feed_second,
    gains,
    gains_first,
    gains_second,
    rel_table,
    table_first,
    table_second,
):
    micro_count, local_rows, width = tokens.shape
    shape = tokens.shape
    seq_size = lax.axis_size("seq")
    seq_len = local_rows * seq_size
    heads_here = HEADS // seq_size
    part = heads_here * HEAD_DIM
    seq_index = lax.axis_index("seq")

    attention_slots = attention_weight.transpose(1, 0, 2)
    feed_slots = feed_weight.transpose(1, 0, 2).astype(jnp.bfloat16)
    attention_mine = to_columns(attention_slots)
    attention_mine, feed_slots = lax.optimization_barrier((attention_mine, feed_slots))
    attention_low = all_rows(attention_mine)
    feed_mine = to_columns(feed_slots)
    weight_out = attention_low[3]

    positions = jnp.arange(seq_len, dtype=jnp.int32)
    buckets = rel_bucket(positions[None, :] - positions[:, None])
    bucket_match = buckets[None, :, :] == jnp.arange(NUM_BUCKETS, dtype=jnp.int32)[:, None, None]
    table_here = lax.dynamic_slice_in_dim(rel_table, seq_index * heads_here, heads_here, 1)
    bias = jnp.einsum(
        "atj,ao->otj",
        bucket_match.astype(jnp.float32),
        table_here,
        precision=HIGHEST,
        preferred_element_type=jnp.float32,
    )

    def as_blocks(matrix):
        return matrix.astype(jnp.bfloat16).reshape(seq_size, micro_count, local_rows, part)

    inputs = tokens.astype(jnp.float32)
    normed_one = gather_tokens(rms_norm(inputs, gains[0]).astype(jnp.bfloat16))
    grad_out = gather_tokens(after(cotangent, normed_one))
    query, key, value = [
        as_blocks(dot(normed_one, attention_low[slot])) for slot in range(3)
    ]
    attended = attention_forward(query, key, value, bias, segments).reshape(-1, part)
    attention_partial, feed_mine, grad_out = lax.optimization_barrier(
        (dot_t(attended, weight_out).astype(jnp.bfloat16), feed_mine, grad_out)
    )
    feed_low = all_rows(feed_mine)
    attention_out = scatter_tokens(attention_partial, shape)
    weight_gate, weight_up, weight_down = feed_low[0], feed_low[1], feed_low[2]
    hidden_state = inputs + attention_out
    normed_two = gather_tokens(rms_norm(hidden_state, gains[1]).astype(jnp.bfloat16))
    gate_pre = dot(normed_two, weight_gate)
    up_pre = dot(normed_two, weight_up)
    gate_act, gate_back = jax.vjp(gelu_tanh, gate_pre)
    inner = (gate_act * up_pre).astype(jnp.bfloat16)
    feed_partial = dot_t(inner, weight_down).astype(jnp.bfloat16)
    grad_inner = dot(grad_out, weight_down)
    grad_gate = gate_back(grad_inner * up_pre)[0].astype(jnp.bfloat16)
    grad_up = (grad_inner * gate_act).astype(jnp.bfloat16)
    grad_normed_two = scatter_tokens(
        dot_t(grad_gate, weight_gate) + dot_t(grad_up, weight_up), shape
    )
    grads_feed = [
        outer_sum(normed_two, grad_gate).astype(jnp.bfloat16),
        outer_sum(normed_two, grad_up).astype(jnp.bfloat16),
        outer_sum(grad_out, inner).astype(jnp.bfloat16),
    ]
    grad_normed_two, grads_feed = lax.optimization_barrier((grad_normed_two, grads_feed))
    feed_first_step = to_rows_first(grads_feed)
    grad_hidden_norm, grad_gain_two = norm_back(hidden_state, gains[1], grad_normed_two)
    grad_hidden = cotangent.astype(jnp.float32) + grad_hidden_norm
    grad_branch = gather_tokens(grad_hidden.astype(jnp.bfloat16))
    grad_branch, feed_partial, feed_first_step = lax.optimization_barrier(
        (grad_branch, feed_partial, feed_first_step)
    )
    block_rows = (hidden_state + scatter_tokens(feed_partial, shape)).astype(jnp.bfloat16)
    grad_attended = as_blocks(dot(grad_branch, weight_out))
    feed_mine_grad = scatter_dp_second(feed_first_step)
    grad_query, grad_key, grad_value, score_sums = attention_backward(
        query, key, value, grad_attended, bias, segments
    )
    grad_query, feed_mine_grad = lax.optimization_barrier((grad_query, feed_mine_grad))
    grad_table_here = jnp.einsum(
        "hij,zij->zh",
        score_sums.astype(jnp.bfloat16),
        bucket_match.astype(jnp.bfloat16),
        preferred_element_type=jnp.float32,
    )
    grad_qkv = [item.reshape(-1, part) for item in (grad_query, grad_key, grad_value)]
    grad_normed_one = scatter_tokens(
        sum(dot_t(grad_qkv[slot], attention_low[slot]) for slot in range(3)), shape
    )
    attention_steps = to_rows_first(
        [outer_sum(normed_one, item) for item in grad_qkv] + [outer_sum(grad_branch, attended)]
    )
    feed_total = to_rows_last(feed_mine_grad).transpose(1, 0, 2)
    attention_total = to_rows_last(scatter_dp_second(attention_steps)).transpose(1, 0, 2)
    grad_input_norm, grad_gain_one = norm_back(inputs, gains[0], grad_normed_one)
    grad_rows = (grad_hidden + grad_input_norm).astype(jnp.bfloat16)
    grad_table = lax.dynamic_update_slice_in_dim(
        jnp.zeros((NUM_BUCKETS, HEADS), jnp.float32), grad_table_here, seq_index * heads_here, 1
    )
    small = jnp.concatenate([grad_gain_one, grad_gain_two, grad_table.reshape(-1)])
    small = sum_all(small.reshape(-1, 128)).reshape(-1)
    gains_total = small[: 2 * width].reshape(2, width)
    table_total = small[2 * width :].reshape(NUM_BUCKETS, HEADS)
    new_attention = adam_update(
        attention_weight,
        attention_first,
        attention_second,
        attention_total,
        attention_rates(),
        DECAY,
    )
    new_feed = adam_update(feed_weight, feed_first, feed_second, feed_total, feed_rates(), DECAY)
    new_gains = adam_update(gains, gains_first, gains_second, gains_total, 0.6, 0.0)
    new_table = adam_update(rel_table, table_first, table_second, table_total, 1.5, 0.0)
    return (
        block_rows,
        grad_rows,
        new_attention[0],
        new_attention[1],
        new_attention[2][:, :3, :],
        new_attention[2][:, 3, :],
        new_feed[0],
        new_feed[1],
        new_feed[2],
        new_gains[0],
        new_gains[1],
        new_gains[2],
        new_table[0],
        new_table[1],
        new_table[2],
    )


def solution(mesh):
    in_specs = (
        P("dp", "seq", None),
        P("dp", None),
        P("dp", "seq", None),
        P(("seq", "dp"), None, None),
        P(("seq", "dp"), None, None),
        P(("seq", "dp"), None, None),
        P(("seq", "dp"), None, None),
        P(("seq", "dp"), None, None),
        P(("seq", "dp"), None, None),
        P(),
        P(),
        P(),
        P(),
        P(),
        P(),
    )
    out_specs = (
        P("dp", "seq", None),
        P("dp", "seq", None),
        P(("seq", "dp"), None, None),
        P(("seq", "dp"), None, None),
        P(("seq", "dp"), None, None),
        P(("seq", "dp"), None),
        P(("seq", "dp"), None, None),
        P(("seq", "dp"), None, None),
        P(("seq", "dp"), None, None),
        P(),
        P(),
        P(),
        P(),
        P(),
        P(),
    )
    return jax.shard_map(local, mesh=mesh, in_specs=in_specs, out_specs=out_specs, check_vma=False)
```

```python
import jax
import jax.numpy as jnp
from jax import lax
from jax.experimental import pallas as pl
from jax.experimental.pallas import tpu as pltpu
from jax.sharding import PartitionSpec as P

D = 2048
HEADS = 32
HEAD_DIM = 64
FF = 5120
NUM_BUCKETS = 32
MAX_DIST = 128
STEP = 10


NORM_EPSILON = 1e-06
NEG_BIG = -1000000000.0
BETA_ONE = 0.9
BETA_TWO = 0.95
EPS_ADAM = 1e-08
DECAY = 0.1
HIGHEST = lax.Precision.HIGHEST


def rms_norm(values, gain_vec):
    inv_root = lax.rsqrt(jnp.mean(values * values, axis=-1, keepdims=True) + NORM_EPSILON)
    return values * inv_root * gain_vec


def gelu_tanh(values):
    return jax.nn.gelu(values, approximate=True)


def bucket_edges():
    half_count = NUM_BUCKETS // 2
    exact_count = half_count // 2
    log_count = half_count - exact_count
    far_ratio = MAX_DIST // exact_count
    edge_list = []
    for step_index in range(1, log_count):
        edge_at = exact_count
        while edge_at**log_count < exact_count**log_count * far_ratio**step_index:
            edge_at = edge_at + 1
        edge_list.append(edge_at)
    return edge_list


def rel_bucket(relative):
    half_count = NUM_BUCKETS // 2
    exact_count = half_count // 2
    distance = jnp.abs(relative)
    far_bucket = jnp.full(relative.shape, exact_count, jnp.int32)
    for edge_at in bucket_edges():
        far_bucket = far_bucket + (distance >= edge_at).astype(jnp.int32)
    near_far = jnp.where(distance < exact_count, distance, far_bucket)
    return near_far + jnp.where(relative > 0, half_count, 0)


def adam_update(weight, first, second, grads, rate, decay):
    first_new = BETA_ONE * first + (1.0 - BETA_ONE) * grads
    second_new = BETA_TWO * second + (1.0 - BETA_TWO) * grads * grads
    first_hat = first_new / (1.0 - BETA_ONE**STEP)
    second_hat = second_new / (1.0 - BETA_TWO**STEP)
    weight_new = weight - rate * (first_hat / (jnp.sqrt(second_hat) + EPS_ADAM) + decay * weight)
    return (weight_new, first_new, second_new)


def attention_rates():
    return 3.0 * jnp.array(
        [D ** (-0.5), (32 * D) ** (-0.5), D ** (-0.5), (HEADS * HEAD_DIM // 64) ** (-0.5)],
        jnp.float32,
    ).reshape(1, 4, 1)


def feed_rates():
    return 3.0 * jnp.array([D ** (-0.5), D ** (-0.5), FF ** (-0.5)], jnp.float32).reshape(1, 3, 1)


def dot(left, right):
    return jnp.dot(left, right, preferred_element_type=jnp.float32)


def dot_t(left, right):
    return lax.dot_general(
        left, right, (((1,), (1,)), ((), ())), preferred_element_type=jnp.float32
    )


def outer_sum(left, right):
    return lax.dot_general(
        left, right, (((0,), (0,)), ((), ())), preferred_element_type=jnp.float32
    )


def norm_stats(values):
    return lax.rsqrt(jnp.mean(values * values, axis=-1, keepdims=True) + NORM_EPSILON)


def norm_back(values, gain_vec, grads):
    inv_root = norm_stats(values)
    unit = values * inv_root
    scaled = grads * gain_vec
    grad_in = inv_root * (scaled - unit * jnp.mean(unit * scaled, axis=-1, keepdims=True))
    return grad_in, jnp.sum(grads * unit, axis=(0, 1))


def partner_pairs(axis, offset):
    return [(index, index ^ offset) for index in range(lax.axis_size(axis))]


def swap(value, axis, offset):
    return lax.ppermute(value, axis, partner_pairs(axis, offset))


MIB = 1024 * 1024
ADAM_PARAMS = pltpu.CompilerParams(vmem_limit_bytes=32 * MIB)


def attention_params(length):
    return pltpu.CompilerParams(vmem_limit_bytes=min(56, length * length // 8192) * MIB)


def adam_values(weight, first, second, grads, rate, decay):
    first_new = BETA_ONE * first + (1.0 - BETA_ONE) * grads
    second_new = BETA_TWO * second + (1.0 - BETA_TWO) * grads * grads
    first_hat = first_new * (1.0 / (1.0 - BETA_ONE**STEP))
    root = jnp.sqrt(second_new * (1.0 / (1.0 - BETA_TWO**STEP)))
    weight_new = weight - rate * (first_hat / (root + EPS_ADAM) + decay * weight)
    return (weight_new, first_new, second_new)


def in_columns(grads):
    seq_size, slots, rows, part = grads.shape
    return wide(grads).transpose(2, 1, 0, 3).reshape(rows, slots, seq_size * part)


def update_attention(weight, first, second, grads):
    seq_size, slots, rows, part = grads.shape
    width = seq_size * part
    if part % 128:
        new = adam_update(weight, first, second, in_columns(grads), attention_rates(), DECAY)
        return new[0], new[1], new[2][:, :3], new[2][:, 3]
    chunk = 2
    scales = [D ** (-0.5), (32 * D) ** (-0.5), D ** (-0.5), (HEADS * HEAD_DIM // 64) ** (-0.5)]

    def body(w_ref, m_ref, v_ref, g_ref, w_out, m_out, v_out, o_out):
        for slot in range(slots):
            for item in range(chunk):
                cols = slice(item * part, (item + 1) * part)
                new = adam_values(
                    w_ref[:, slot, cols],
                    m_ref[:, slot, cols],
                    v_ref[:, slot, cols],
                    wide(g_ref[item, slot]),
                    3.0 * scales[slot],
                    DECAY,
                )
                w_out[:, slot, cols] = new[0]
                m_out[:, slot, cols] = new[1]
                if slot < slots - 1:
                    v_out[slot, :, cols] = new[2]
                else:
                    o_out[:, cols] = new[2]

    state_spec = pl.BlockSpec((rows, slots, chunk * part), lambda j: (0, 0, j))
    new = pl.pallas_call(
        body,
        grid=(seq_size // chunk,),
        in_specs=[state_spec] * 3
        + [pl.BlockSpec((chunk, slots, rows, part), lambda j: (j, 0, 0, 0))],
        out_specs=[
            state_spec,
            state_spec,
            pl.BlockSpec((slots - 1, rows, chunk * part), lambda j: (0, 0, j)),
            pl.BlockSpec((rows, chunk * part), lambda j: (0, j)),
        ],
        out_shape=[
            jax.ShapeDtypeStruct(weight.shape, jnp.float32),
            jax.ShapeDtypeStruct(weight.shape, jnp.float32),
            jax.ShapeDtypeStruct((slots - 1, rows, width), jnp.float32),
            jax.ShapeDtypeStruct((rows, width), jnp.float32),
        ],
        compiler_params=ADAM_PARAMS,
        cost_estimate=pl.CostEstimate(
            flops=20 * weight.size, bytes_accessed=26 * weight.size, transcendentals=weight.size
        ),
    )(weight, first, second, grads)
    return new[0], new[1], new[2].transpose(1, 0, 2), new[3]


def update_feed(weight, first, second, grads):
    seq_size, slots, rows, part = grads.shape
    if part % 128:
        return adam_update(weight, first, second, in_columns(grads), feed_rates(), DECAY)

    def body(w_ref, m_ref, v_ref, g_ref, w_out, m_out, v_out):
        rate = jnp.where(pl.program_id(0) == slots - 1, 3.0 * FF ** (-0.5), 3.0 * D ** (-0.5))
        for item in range(chunk):
            cols = slice(item * part, (item + 1) * part)
            new = adam_values(
                w_ref[0, :, cols],
                m_ref[0, :, cols],
                v_ref[0, :, cols],
                wide(g_ref[item, 0]),
                rate,
                DECAY,
            )
            for ref, value in zip((w_out, m_out, v_out), new):
                ref[0, :, cols] = value

    chunk = 4
    state_spec = pl.BlockSpec((1, rows, chunk * part), lambda slot, j: (slot, 0, j))
    state = [item.transpose(1, 0, 2) for item in (weight, first, second)]
    new = pl.pallas_call(
        body,
        grid=(slots, seq_size // chunk),
        in_specs=[state_spec] * 3
        + [pl.BlockSpec((chunk, 1, rows, part), lambda slot, j: (j, slot, 0, 0))],
        out_specs=[state_spec] * 3,
        out_shape=[jax.ShapeDtypeStruct(state[0].shape, jnp.float32)] * 3,
        compiler_params=ADAM_PARAMS,
        cost_estimate=pl.CostEstimate(
            flops=20 * weight.size, bytes_accessed=26 * weight.size, transcendentals=weight.size
        ),
    )(*state, grads)
    return [item.transpose(1, 0, 2) for item in new]


def head_probs(query, key, bias, same_doc):
    scores = lax.dot_general(
        query, key, (((1,), (1,)), ((), ())), preferred_element_type=jnp.float32
    )
    scores = jnp.where(same_doc, scores + bias, NEG_BIG)
    exp_scores = jnp.exp(scores - jnp.max(scores, axis=-1, keepdims=True))
    return exp_scores * (1.0 / jnp.sum(exp_scores, axis=-1, keepdims=True))


def attention_specs(seq_size, rows):
    length = seq_size * rows
    tokens_spec = pl.BlockSpec((seq_size, 1, rows, 128), lambda pair, m: (0, m, 0, pair))
    return tokens_spec, [
        pl.BlockSpec((2, length, length), lambda pair, m: (pair, 0, 0)),
        pl.BlockSpec((1, length, 1), lambda pair, m: (m, 0, 0)),
        pl.BlockSpec((1, 1, length), lambda pair, m: (m, 0, 0)),
    ]


def attention_forward(query, key, value, bias, segments):
    seq_size, micro_count, rows, part = query.shape
    length = seq_size * rows
    tokens_spec, other_specs = attention_specs(seq_size, rows)

    def body(q_ref, k_ref, v_ref, bias_ref, seg_q_ref, seg_k_ref, out_ref):
        q, k, v = [ref[:, 0].reshape(length, 128) for ref in (q_ref, k_ref, v_ref)]
        same_doc = seg_q_ref[0] == seg_k_ref[0]
        outs = []
        for h in range(2):
            cols = slice(h * HEAD_DIM, (h + 1) * HEAD_DIM)
            probs = head_probs(q[:, cols], k[:, cols], bias_ref[h], same_doc)
            outs.append(dot(probs.astype(jnp.bfloat16), v[:, cols]))
        out = jnp.concatenate(outs, 1).astype(jnp.bfloat16)
        out_ref[...] = out.reshape(seq_size, 1, rows, 128)

    return pl.pallas_call(
        body,
        grid=(part // 128, micro_count),
        in_specs=[tokens_spec] * 3 + other_specs,
        out_specs=tokens_spec,
        out_shape=jax.ShapeDtypeStruct(query.shape, jnp.bfloat16),
        compiler_params=attention_params(length),
        cost_estimate=pl.CostEstimate(
            flops=6000 * length * query.size // HEAD_DIM,
            bytes_accessed=8 * query.size + bias.size * 4,
            transcendentals=length * query.size // HEAD_DIM,
        ),
    )(query, key, value, bias, segments[:, :, None], segments[:, None, :])


def attention_backward(query, key, value, grad_out, bias, segments):
    seq_size, micro_count, rows, part = query.shape
    length = seq_size * rows
    tokens_spec, other_specs = attention_specs(seq_size, rows)

    def body(
        q_ref, k_ref, v_ref, g_ref, bias_ref, seg_q_ref, seg_k_ref, dq_ref, dk_ref, dv_ref, ds_ref
    ):
        q, k, v, g = [ref[:, 0].reshape(length, 128) for ref in (q_ref, k_ref, v_ref, g_ref)]
        same_doc = seg_q_ref[0] == seg_k_ref[0]
        first = pl.program_id(1) == 0
        grads = ([], [], [])
        for h in range(2):
            cols = slice(h * HEAD_DIM, (h + 1) * HEAD_DIM)
            probs = head_probs(q[:, cols], k[:, cols], bias_ref[h], same_doc)
            grad_probs = dot_t(g[:, cols], v[:, cols])
            row_dot = jnp.sum(probs * grad_probs, axis=-1, keepdims=True)
            grad_scores = (probs * (grad_probs - row_dot)).astype(jnp.bfloat16)
            wide = grad_scores.astype(jnp.float32)
            ds_ref[h] = jnp.where(first, wide, ds_ref[h] + wide)
            grads[0].append(dot(grad_scores, k[:, cols]))
            grads[1].append(outer_sum(grad_scores, q[:, cols]))
            grads[2].append(outer_sum(probs.astype(jnp.bfloat16), g[:, cols]))
        for ref, parts in zip((dq_ref, dk_ref, dv_ref), grads):
            joined = jnp.concatenate(parts, 1).astype(jnp.bfloat16)
            ref[...] = joined.reshape(seq_size, 1, rows, 128)

    return pl.pallas_call(
        body,
        grid=(part // 128, micro_count),
        in_specs=[tokens_spec] * 4 + other_specs,
        out_specs=[tokens_spec] * 3
        + [pl.BlockSpec((2, length, length), lambda pair, m: (pair, 0, 0))],
        out_shape=[jax.ShapeDtypeStruct(query.shape, jnp.bfloat16)] * 3
        + [jax.ShapeDtypeStruct((part // HEAD_DIM, length, length), jnp.float32)],
        compiler_params=attention_params(length),
        cost_estimate=pl.CostEstimate(
            flops=8000 * length * query.size // HEAD_DIM,
            bytes_accessed=14 * query.size + bias.size * 8,
            transcendentals=length * query.size // HEAD_DIM,
        ),
    )(query, key, value, grad_out, bias, segments[:, :, None], segments[:, None, :])


def gather_dp_first(mine):
    if lax.axis_size("dp") != 4:
        return [lax.all_gather(mine, "dp", axis=2)]
    return [mine, swap(mine, "dp", 1), swap(mine, "dp", 2)]


def gather_dp_second(items):
    if len(items) == 1:
        full = items[0]
    else:
        mine, one, two = items
        me = lax.axis_index("dp")
        half = mine.shape[1] // 2
        low = swap(one[:, :half], "dp", 2)
        high = swap(two[:, half:], "dp", 1)
        full = jnp.zeros(mine.shape[:2] + (4,) + mine.shape[2:], mine.dtype)
        for piece, source, start in (
            (mine, 0, 0),
            (one, 1, 0),
            (two, 2, 0),
            (low, 3, 0),
            (high, 3, half),
        ):
            full = lax.dynamic_update_slice(full, piece[:, :, None], (0, start, me ^ source, 0, 0))
    return full.reshape(full.shape[0], -1, full.shape[-1])


def wide(value):
    return value.astype(jnp.float32)


def scatter_dp_first(partial):
    if lax.axis_size("dp") != 4:
        return [lax.psum_scatter(partial, "dp", scatter_dimension=2)]
    me = lax.axis_index("dp")
    half = partial.shape[1] // 2
    pieces = [lax.dynamic_index_in_dim(partial, me ^ k, 2, keepdims=False) for k in range(4)]
    low = [piece[:, :half] for piece in pieces]
    high = [piece[:, half:] for piece in pieces]
    return low[:3] + high[:3] + [swap(low[3], "dp", 1), swap(high[3], "dp", 2)]


def scatter_dp_second(items):
    if len(items) == 1:
        return items
    low = items[:3]
    high = items[3:6]
    low_two = (wide(low[2]) + wide(items[6])).astype(jnp.bfloat16)
    high_one = (wide(high[1]) + wide(items[7])).astype(jnp.bfloat16)
    return [low[0], high[0], swap(low[1], "dp", 1), swap(high[2], "dp", 2), low_two, high_one]


def scatter_dp_third(items):
    if len(items) == 1:
        return items[0]
    low, high, low_more, high_more, low_two, high_one = items
    low_sum = wide(low) + wide(low_more) + wide(swap(low_two, "dp", 2))
    high_sum = wide(high) + wide(high_more) + wide(swap(high_one, "dp", 1))
    return jnp.concatenate([low_sum, high_sum], 1).astype(jnp.bfloat16)


def to_columns(weight):
    seq_size = lax.axis_size("seq")
    slots, rows, width = weight.shape
    send = weight.reshape(slots, rows, seq_size, width // seq_size).transpose(2, 0, 1, 3)
    return lax.all_to_all(send, "seq", 0, 0).transpose(1, 0, 2, 3)


def to_rows(mine):
    return lax.all_to_all(mine.transpose(1, 0, 2, 3), "seq", 0, 0)


def after(value, *earlier):
    return lax.optimization_barrier((value,) + earlier)[0]


def to_rows_first(grads):
    seq_size = lax.axis_size("seq")
    dp_size = lax.axis_size("dp")
    partial = jnp.stack([grad.astype(jnp.bfloat16) for grad in grads], 0)
    slots, total, part = partial.shape
    rows = total // (seq_size * dp_size)
    return scatter_dp_first(partial.reshape(slots, seq_size, dp_size, rows, part))


def sum_all(value):
    for axis in ("seq", "dp"):
        offset = 1
        while offset < lax.axis_size(axis):
            value = value + swap(value, axis, offset)
            offset = offset * 2
    return value


def gather_tokens(local_rows):
    full = lax.all_gather(local_rows, "seq", axis=0)
    return full.reshape(-1, local_rows.shape[-1])


def scatter_tokens(partial, shape):
    send = partial.astype(jnp.bfloat16).reshape((lax.axis_size("seq"),) + shape)
    return lax.psum_scatter(send, "seq", scatter_dimension=0).astype(jnp.float32)


def local(
    tokens,
    segments,
    cotangent,
    attention_weight,
    attention_first,
    attention_second,
    feed_weight,
    feed_first,
    feed_second,
    gains,
    gains_first,
    gains_second,
    rel_table,
    table_first,
    table_second,
):
    micro_count, local_rows, width = tokens.shape
    shape = tokens.shape
    seq_size = lax.axis_size("seq")
    seq_len = local_rows * seq_size
    heads_here = HEADS // seq_size
    part = heads_here * HEAD_DIM
    seq_index = lax.axis_index("seq")

    attention_slots = attention_weight.transpose(1, 0, 2).astype(jnp.bfloat16)
    feed_slots = feed_weight.transpose(1, 0, 2).astype(jnp.bfloat16)
    inputs = tokens.astype(jnp.float32)
    normed_here = rms_norm(inputs, gains[0]).astype(jnp.bfloat16)
    attention_mine, normed_here = lax.optimization_barrier(
        (to_columns(attention_slots), normed_here)
    )
    normed_one = gather_tokens(normed_here)
    attention_items, late_cotangent = lax.optimization_barrier(
        (gather_dp_first(attention_mine), cotangent)
    )
    attention_low = gather_dp_second(attention_items)
    weight_out = attention_low[3]

    positions = jnp.arange(seq_len, dtype=jnp.int32)
    buckets = rel_bucket(positions[None, :] - positions[:, None])
    bucket_match = buckets[None, :, :] == jnp.arange(NUM_BUCKETS, dtype=jnp.int32)[:, None, None]
    table_here = lax.dynamic_slice_in_dim(rel_table, seq_index * heads_here, heads_here, 1)
    bias = jnp.einsum(
        "atj,ao->otj",
        bucket_match.astype(jnp.float32),
        table_here,
        precision=HIGHEST,
        preferred_element_type=jnp.float32,
    )

    def as_blocks(matrix):
        return matrix.astype(jnp.bfloat16).reshape(seq_size, micro_count, local_rows, part)

    grad_out = gather_tokens(late_cotangent)
    query, key, value = [
        as_blocks(dot(normed_one, attention_low[slot])) for slot in range(3)
    ]
    query, key, value, feed_slots = lax.optimization_barrier((query, key, value, feed_slots))
    feed_mine = to_columns(feed_slots)
    attended = attention_forward(query, key, value, bias, segments).reshape(-1, part)
    attention_partial, grad_out, feed_mine = lax.optimization_barrier(
        (dot_t(attended, weight_out).astype(jnp.bfloat16), grad_out, feed_mine)
    )
    feed_gathered = gather_dp_first(feed_mine)
    attention_out = scatter_tokens(attention_partial, shape)
    attention_out, feed_gathered = lax.optimization_barrier((attention_out, feed_gathered))
    feed_low = gather_dp_second(feed_gathered)
    weight_gate, weight_up, weight_down = feed_low[0], feed_low[1], feed_low[2]
    hidden_state = inputs + attention_out
    normed_two = gather_tokens(rms_norm(hidden_state, gains[1]).astype(jnp.bfloat16))
    gate_pre = dot(normed_two, weight_gate)
    up_pre = dot(normed_two, weight_up)
    gate_act, gate_back = jax.vjp(gelu_tanh, gate_pre)
    inner = (gate_act * up_pre).astype(jnp.bfloat16)
    feed_partial = dot_t(inner, weight_down).astype(jnp.bfloat16)
    grad_inner = dot(grad_out, weight_down)
    grad_gate = gate_back(grad_inner * up_pre)[0].astype(jnp.bfloat16)
    grad_up = (grad_inner * gate_act).astype(jnp.bfloat16)
    grad_normed_two = scatter_tokens(
        dot_t(grad_gate, weight_gate) + dot_t(grad_up, weight_up), shape
    )
    grads_feed = [
        outer_sum(normed_two, grad_gate).astype(jnp.bfloat16),
        outer_sum(normed_two, grad_up).astype(jnp.bfloat16),
        outer_sum(grad_out, inner).astype(jnp.bfloat16),
    ]
    feed_steps = to_rows_first(grads_feed)
    grad_normed_two, feed_steps = lax.optimization_barrier((grad_normed_two, feed_steps))
    feed_steps = scatter_dp_second(feed_steps)
    grad_hidden_norm, grad_gain_two = norm_back(hidden_state, gains[1], grad_normed_two)
    grad_hidden = cotangent.astype(jnp.float32) + grad_hidden_norm
    grad_branch = gather_tokens(grad_hidden.astype(jnp.bfloat16))
    grad_branch, feed_mine_grad = lax.optimization_barrier(
        (grad_branch, scatter_dp_third(feed_steps))
    )
    grad_attended = as_blocks(dot(grad_branch, weight_out))
    feed_total = to_rows(feed_mine_grad)
    grad_query, grad_key, grad_value, score_sums = attention_backward(
        query, key, value, grad_attended, bias, segments
    )
    grad_table_here = jnp.einsum(
        "hij,zij->zh",
        score_sums.astype(jnp.bfloat16),
        bucket_match.astype(jnp.bfloat16),
        preferred_element_type=jnp.float32,
    )
    grad_qkv = [item.reshape(-1, part) for item in (grad_query, grad_key, grad_value)]
    normed_partial = sum(dot_t(grad_qkv[slot], attention_low[slot]) for slot in range(3))
    normed_partial, feed_total = lax.optimization_barrier(
        (normed_partial.astype(jnp.bfloat16), feed_total)
    )
    grad_normed_one = scatter_tokens(normed_partial, shape)
    block_rows = hidden_state + scatter_tokens(after(feed_partial, grad_normed_one), shape)
    block_rows = block_rows.astype(jnp.bfloat16)
    attention_steps = to_rows_first(
        [outer_sum(normed_one, item) for item in grad_qkv] + [outer_sum(grad_branch, attended)]
    )
    attention_total = to_rows(scatter_dp_third(scatter_dp_second(attention_steps)))
    grad_input_norm, grad_gain_one = norm_back(inputs, gains[0], grad_normed_one)
    grad_rows = (grad_hidden + grad_input_norm).astype(jnp.bfloat16)
    grad_table = lax.dynamic_update_slice_in_dim(
        jnp.zeros((NUM_BUCKETS, HEADS), jnp.float32), grad_table_here, seq_index * heads_here, 1
    )
    small = jnp.concatenate([grad_gain_one, grad_gain_two, grad_table.reshape(-1)])
    small = sum_all(small.reshape(-1, 128)).reshape(-1)
    gains_total = small[: 2 * width].reshape(2, width)
    table_total = small[2 * width :].reshape(NUM_BUCKETS, HEADS)
    new_attention = update_attention(
        attention_weight, attention_first, attention_second, attention_total
    )
    new_feed = update_feed(feed_weight, feed_first, feed_second, feed_total)
    new_gains = adam_update(gains, gains_first, gains_second, gains_total, 0.6, 0.0)
    new_table = adam_update(rel_table, table_first, table_second, table_total, 1.5, 0.0)
    return (
        block_rows,
        grad_rows,
        new_attention[0],
        new_attention[1],
        new_attention[2],
        new_attention[3],
        new_feed[0],
        new_feed[1],
        new_feed[2],
        new_gains[0],
        new_gains[1],
        new_gains[2],
        new_table[0],
        new_table[1],
        new_table[2],
    )


def solution(mesh):
    in_specs = (
        P("dp", "seq", None),
        P("dp", None),
        P("dp", "seq", None),
        P(("seq", "dp"), None, None),
        P(("seq", "dp"), None, None),
        P(("seq", "dp"), None, None),
        P(("seq", "dp"), None, None),
        P(("seq", "dp"), None, None),
        P(("seq", "dp"), None, None),
        P(),
        P(),
        P(),
        P(),
        P(),
        P(),
    )
    out_specs = (
        P("dp", "seq", None),
        P("dp", "seq", None),
        P(("seq", "dp"), None, None),
        P(("seq", "dp"), None, None),
        P(("seq", "dp"), None, None),
        P(("seq", "dp"), None),
        P(("seq", "dp"), None, None),
        P(("seq", "dp"), None, None),
        P(("seq", "dp"), None, None),
        P(),
        P(),
        P(),
        P(),
        P(),
        P(),
    )
    return jax.shard_map(local, mesh=mesh, in_specs=in_specs, out_specs=out_specs, check_vma=False)
```

```python
import math

import jax
import jax.numpy as jnp
from jax import lax
from jax.experimental import pallas as pl
from jax.experimental.pallas import tpu as pltpu
from jax.sharding import PartitionSpec as P

D = 2048
HEADS = 32
HEAD_DIM = 64
FF = 5120
NUM_BUCKETS = 32
MAX_DIST = 128
STEP = 10


NORM_EPSILON = 1e-06
NEG_BIG = -1000000000.0
BETA_ONE = 0.9
BETA_TWO = 0.95
EPS_ADAM = 1e-08
DECAY = 0.1
HIGHEST = lax.Precision.HIGHEST


def rms_norm(values, gain_vec):
    inv_root = lax.rsqrt(jnp.mean(values * values, axis=-1, keepdims=True) + NORM_EPSILON)
    return values * inv_root * gain_vec


def bucket_edges():
    half_count = NUM_BUCKETS // 2
    exact_count = half_count // 2
    log_count = half_count - exact_count
    far_ratio = MAX_DIST // exact_count
    edge_list = []
    for step_index in range(1, log_count):
        edge_at = exact_count
        while edge_at**log_count < exact_count**log_count * far_ratio**step_index:
            edge_at = edge_at + 1
        edge_list.append(edge_at)
    return edge_list


def rel_bucket(relative):
    half_count = NUM_BUCKETS // 2
    exact_count = half_count // 2
    distance = jnp.abs(relative)
    far_bucket = jnp.full(relative.shape, exact_count, jnp.int32)
    for edge_at in bucket_edges():
        far_bucket = far_bucket + (distance >= edge_at).astype(jnp.int32)
    near_far = jnp.where(distance < exact_count, distance, far_bucket)
    return near_far + jnp.where(relative > 0, half_count, 0)


def adam_update(weight, first, second, grads, rate, decay):
    first_new = BETA_ONE * first + (1.0 - BETA_ONE) * grads
    second_new = BETA_TWO * second + (1.0 - BETA_TWO) * grads * grads
    first_hat = first_new / (1.0 - BETA_ONE**STEP)
    second_hat = second_new / (1.0 - BETA_TWO**STEP)
    weight_new = weight - rate * (first_hat / (jnp.sqrt(second_hat) + EPS_ADAM) + decay * weight)
    return (weight_new, first_new, second_new)


def attention_rates():
    return 3.0 * jnp.array(
        [D ** (-0.5), (32 * D) ** (-0.5), D ** (-0.5), (HEADS * HEAD_DIM // 64) ** (-0.5)],
        jnp.float32,
    ).reshape(1, 4, 1)


def feed_rates():
    return 3.0 * jnp.array([D ** (-0.5), D ** (-0.5), FF ** (-0.5)], jnp.float32).reshape(1, 3, 1)


def dot(left, right):
    return jnp.dot(left, right, preferred_element_type=jnp.float32)


def dot_t(left, right):
    return lax.dot_general(
        left, right, (((1,), (1,)), ((), ())), preferred_element_type=jnp.float32
    )


def outer_sum(left, right):
    return lax.dot_general(
        left, right, (((0,), (0,)), ((), ())), preferred_element_type=jnp.float32
    )


def norm_stats(values):
    return lax.rsqrt(jnp.mean(values * values, axis=-1, keepdims=True) + NORM_EPSILON)


def norm_back(values, gain_vec, grads):
    inv_root = norm_stats(values)
    unit = values * inv_root
    scaled = grads * gain_vec
    grad_in = inv_root * (scaled - unit * jnp.mean(unit * scaled, axis=-1, keepdims=True))
    return grad_in, jnp.sum(grads * unit, axis=(0, 1))


def feed_middle(normed, grad_inner, weight_gate, weight_up):
    tokens, width = normed.shape
    hidden = weight_gate.shape[1]
    block = 256
    scale = (2.0 / math.pi) ** 0.5

    def body(n_ref, gi_ref, wg_ref, wu_ref, inner_ref, gg_ref, gu_ref, out_ref):
        gate = dot(n_ref[...], wg_ref[...])
        up = dot(n_ref[...], wu_ref[...])
        grad_inner = gi_ref[...]
        squared = gate * gate
        tanh = jnp.tanh(scale * (gate + 0.044715 * (squared * gate)))
        half = 0.5 * (1.0 + tanh)
        act = gate * half
        slope = half + 0.5 * gate * (1.0 - tanh * tanh) * (scale * (1.0 + 0.134145 * squared))
        inner_ref[...] = (act * up).astype(jnp.bfloat16)
        grad_gate = (grad_inner * up * slope).astype(jnp.bfloat16)
        grad_up = (grad_inner * act).astype(jnp.bfloat16)
        gg_ref[...] = grad_gate
        gu_ref[...] = grad_up
        total = dot_t(grad_gate, wg_ref[...]) + dot_t(grad_up, wu_ref[...])
        out_ref[...] = total.astype(jnp.bfloat16)

    rows = pl.BlockSpec((block, width), lambda i: (i, 0))
    units = pl.BlockSpec((block, hidden), lambda i: (i, 0))
    weights = pl.BlockSpec((width, hidden), lambda i: (0, 0))
    low_units = jax.ShapeDtypeStruct((tokens, hidden), jnp.bfloat16)
    return pl.pallas_call(
        body,
        grid=(tokens // block,),
        in_specs=[rows, units, weights, weights],
        out_specs=[units, units, units, rows],
        out_shape=[
            low_units,
            low_units,
            low_units,
            jax.ShapeDtypeStruct((tokens, width), jnp.bfloat16),
        ],
        compiler_params=pltpu.CompilerParams(vmem_limit_bytes=40 * MIB),
        cost_estimate=pl.CostEstimate(
            flops=8 * tokens * width * hidden,
            bytes_accessed=4 * tokens * width + 10 * tokens * hidden + 4 * width * hidden,
            transcendentals=tokens * hidden,
        ),
    )(normed, grad_inner, weight_gate, weight_up)


def partner_pairs(axis, offset):
    return [(index, index ^ offset) for index in range(lax.axis_size(axis))]


def swap(value, axis, offset):
    return lax.ppermute(value, axis, partner_pairs(axis, offset))


MIB = 1024 * 1024
ADAM_PARAMS = pltpu.CompilerParams(vmem_limit_bytes=32 * MIB)


def attention_params(length):
    return pltpu.CompilerParams(vmem_limit_bytes=min(56, length * length // 8192) * MIB)


def adam_values(weight, first, second, grads, rate, decay):
    first_new = BETA_ONE * first + (1.0 - BETA_ONE) * grads
    second_new = BETA_TWO * second + (1.0 - BETA_TWO) * grads * grads
    first_hat = first_new * (1.0 / (1.0 - BETA_ONE**STEP))
    root = jnp.sqrt(second_new * (1.0 / (1.0 - BETA_TWO**STEP)))
    weight_new = weight - rate * (first_hat / (root + EPS_ADAM) + decay * weight)
    return (weight_new, first_new, second_new)


def in_columns(grads):
    seq_size, slots, rows, part = grads.shape
    return wide(grads).transpose(2, 1, 0, 3).reshape(rows, slots, seq_size * part)


def update_attention(weight, first, second, grads):
    seq_size, slots, rows, part = grads.shape
    width = seq_size * part
    if part % 128:
        new = adam_update(weight, first, second, in_columns(grads), attention_rates(), DECAY)
        return new[0], new[1], new[2][:, :3], new[2][:, 3]
    chunk = 2
    scales = [D ** (-0.5), (32 * D) ** (-0.5), D ** (-0.5), (HEADS * HEAD_DIM // 64) ** (-0.5)]

    def body(w_ref, m_ref, v_ref, g_ref, w_out, m_out, v_out, o_out):
        for slot in range(slots):
            for item in range(chunk):
                cols = slice(item * part, (item + 1) * part)
                new = adam_values(
                    w_ref[:, slot, cols],
                    m_ref[:, slot, cols],
                    v_ref[:, slot, cols],
                    wide(g_ref[item, slot]),
                    3.0 * scales[slot],
                    DECAY,
                )
                w_out[:, slot, cols] = new[0]
                m_out[:, slot, cols] = new[1]
                if slot < slots - 1:
                    v_out[slot, :, cols] = new[2]
                else:
                    o_out[:, cols] = new[2]

    state_spec = pl.BlockSpec((rows, slots, chunk * part), lambda j: (0, 0, j))
    new = pl.pallas_call(
        body,
        grid=(seq_size // chunk,),
        in_specs=[state_spec] * 3
        + [pl.BlockSpec((chunk, slots, rows, part), lambda j: (j, 0, 0, 0))],
        out_specs=[
            state_spec,
            state_spec,
            pl.BlockSpec((slots - 1, rows, chunk * part), lambda j: (0, 0, j)),
            pl.BlockSpec((rows, chunk * part), lambda j: (0, j)),
        ],
        out_shape=[
            jax.ShapeDtypeStruct(weight.shape, jnp.float32),
            jax.ShapeDtypeStruct(weight.shape, jnp.float32),
            jax.ShapeDtypeStruct((slots - 1, rows, width), jnp.float32),
            jax.ShapeDtypeStruct((rows, width), jnp.float32),
        ],
        compiler_params=ADAM_PARAMS,
        cost_estimate=pl.CostEstimate(
            flops=20 * weight.size, bytes_accessed=26 * weight.size, transcendentals=weight.size
        ),
    )(weight, first, second, grads)
    return new[0], new[1], new[2].transpose(1, 0, 2), new[3]


def update_feed(weight, first, second, grads):
    seq_size, slots, rows, part = grads.shape
    if part % 128:
        return adam_update(weight, first, second, in_columns(grads), feed_rates(), DECAY)

    def body(w_ref, m_ref, v_ref, g_ref, w_out, m_out, v_out):
        rate = jnp.where(pl.program_id(0) == slots - 1, 3.0 * FF ** (-0.5), 3.0 * D ** (-0.5))
        for item in range(chunk):
            cols = slice(item * part, (item + 1) * part)
            new = adam_values(
                w_ref[0, :, cols],
                m_ref[0, :, cols],
                v_ref[0, :, cols],
                wide(g_ref[item, 0]),
                rate,
                DECAY,
            )
            for ref, value in zip((w_out, m_out, v_out), new):
                ref[0, :, cols] = value

    chunk = 4
    state_spec = pl.BlockSpec((1, rows, chunk * part), lambda slot, j: (slot, 0, j))
    state = [item.transpose(1, 0, 2) for item in (weight, first, second)]
    new = pl.pallas_call(
        body,
        grid=(slots, seq_size // chunk),
        in_specs=[state_spec] * 3
        + [pl.BlockSpec((chunk, 1, rows, part), lambda slot, j: (j, slot, 0, 0))],
        out_specs=[state_spec] * 3,
        out_shape=[jax.ShapeDtypeStruct(state[0].shape, jnp.float32)] * 3,
        compiler_params=ADAM_PARAMS,
        cost_estimate=pl.CostEstimate(
            flops=20 * weight.size, bytes_accessed=26 * weight.size, transcendentals=weight.size
        ),
    )(*state, grads)
    return [item.transpose(1, 0, 2) for item in new]


def head_probs(query, key, bias, same_doc):
    scores = lax.dot_general(
        query, key, (((1,), (1,)), ((), ())), preferred_element_type=jnp.float32
    )
    scores = jnp.where(same_doc, scores + bias, NEG_BIG)
    exp_scores = jnp.exp(scores - jnp.max(scores, axis=-1, keepdims=True))
    return exp_scores * (1.0 / jnp.sum(exp_scores, axis=-1, keepdims=True))


def attention_specs(seq_size, rows):
    length = seq_size * rows
    tokens_spec = pl.BlockSpec((seq_size, 1, rows, 128), lambda pair, m: (0, m, 0, pair))
    return tokens_spec, [
        pl.BlockSpec((2, length, length), lambda pair, m: (pair, 0, 0)),
        pl.BlockSpec((1, length, 1), lambda pair, m: (m, 0, 0)),
        pl.BlockSpec((1, 1, length), lambda pair, m: (m, 0, 0)),
    ]


def attention_forward(query, key, value, bias, segments):
    seq_size, micro_count, rows, part = query.shape
    length = seq_size * rows
    tokens_spec, other_specs = attention_specs(seq_size, rows)

    def body(q_ref, k_ref, v_ref, bias_ref, seg_q_ref, seg_k_ref, out_ref):
        q, k, v = [ref[:, 0].reshape(length, 128) for ref in (q_ref, k_ref, v_ref)]
        same_doc = seg_q_ref[0] == seg_k_ref[0]
        outs = []
        for h in range(2):
            cols = slice(h * HEAD_DIM, (h + 1) * HEAD_DIM)
            probs = head_probs(q[:, cols], k[:, cols], bias_ref[h], same_doc)
            outs.append(dot(probs.astype(jnp.bfloat16), v[:, cols]))
        out = jnp.concatenate(outs, 1).astype(jnp.bfloat16)
        out_ref[...] = out.reshape(seq_size, 1, rows, 128)

    return pl.pallas_call(
        body,
        grid=(part // 128, micro_count),
        in_specs=[tokens_spec] * 3 + other_specs,
        out_specs=tokens_spec,
        out_shape=jax.ShapeDtypeStruct(query.shape, jnp.bfloat16),
        compiler_params=attention_params(length),
        cost_estimate=pl.CostEstimate(
            flops=6000 * length * query.size // HEAD_DIM,
            bytes_accessed=8 * query.size + bias.size * 4,
            transcendentals=length * query.size // HEAD_DIM,
        ),
    )(query, key, value, bias, segments[:, :, None], segments[:, None, :])


def attention_backward(query, key, value, grad_out, bias, segments):
    seq_size, micro_count, rows, part = query.shape
    length = seq_size * rows
    tokens_spec, other_specs = attention_specs(seq_size, rows)

    def body(
        q_ref, k_ref, v_ref, g_ref, bias_ref, seg_q_ref, seg_k_ref, dq_ref, dk_ref, dv_ref, ds_ref
    ):
        q, k, v, g = [ref[:, 0].reshape(length, 128) for ref in (q_ref, k_ref, v_ref, g_ref)]
        same_doc = seg_q_ref[0] == seg_k_ref[0]
        first = pl.program_id(1) == 0
        grads = ([], [], [])
        for h in range(2):
            cols = slice(h * HEAD_DIM, (h + 1) * HEAD_DIM)
            probs = head_probs(q[:, cols], k[:, cols], bias_ref[h], same_doc)
            grad_probs = dot_t(g[:, cols], v[:, cols])
            row_dot = jnp.sum(probs * grad_probs, axis=-1, keepdims=True)
            grad_scores = (probs * (grad_probs - row_dot)).astype(jnp.bfloat16)
            wide = grad_scores.astype(jnp.float32)
            ds_ref[h] = jnp.where(first, wide, ds_ref[h] + wide)
            grads[0].append(dot(grad_scores, k[:, cols]))
            grads[1].append(outer_sum(grad_scores, q[:, cols]))
            grads[2].append(outer_sum(probs.astype(jnp.bfloat16), g[:, cols]))
        for ref, parts in zip((dq_ref, dk_ref, dv_ref), grads):
            joined = jnp.concatenate(parts, 1).astype(jnp.bfloat16)
            ref[...] = joined.reshape(seq_size, 1, rows, 128)

    return pl.pallas_call(
        body,
        grid=(part // 128, micro_count),
        in_specs=[tokens_spec] * 4 + other_specs,
        out_specs=[tokens_spec] * 3
        + [pl.BlockSpec((2, length, length), lambda pair, m: (pair, 0, 0))],
        out_shape=[jax.ShapeDtypeStruct(query.shape, jnp.bfloat16)] * 3
        + [jax.ShapeDtypeStruct((part // HEAD_DIM, length, length), jnp.float32)],
        compiler_params=attention_params(length),
        cost_estimate=pl.CostEstimate(
            flops=8000 * length * query.size // HEAD_DIM,
            bytes_accessed=14 * query.size + bias.size * 8,
            transcendentals=length * query.size // HEAD_DIM,
        ),
    )(query, key, value, grad_out, bias, segments[:, :, None], segments[:, None, :])


def gather_dp_first(mine):
    if lax.axis_size("dp") != 4:
        return [lax.all_gather(mine, "dp", axis=2)]
    return [mine, swap(mine, "dp", 1), swap(mine, "dp", 2)]


def gather_dp_second(items):
    if len(items) == 1:
        full = items[0]
    else:
        mine, one, two = items
        me = lax.axis_index("dp")
        half = mine.shape[1] // 2
        low = swap(one[:, :half], "dp", 2)
        high = swap(two[:, half:], "dp", 1)
        full = jnp.zeros(mine.shape[:2] + (4,) + mine.shape[2:], mine.dtype)
        for piece, source, start in (
            (mine, 0, 0),
            (one, 1, 0),
            (two, 2, 0),
            (low, 3, 0),
            (high, 3, half),
        ):
            full = lax.dynamic_update_slice(full, piece[:, :, None], (0, start, me ^ source, 0, 0))
    return full.reshape(full.shape[0], -1, full.shape[-1])


def wide(value):
    return value.astype(jnp.float32)


def scatter_dp_first(partial):
    if lax.axis_size("dp") != 4:
        return [lax.psum_scatter(partial, "dp", scatter_dimension=2)]
    me = lax.axis_index("dp")
    half = partial.shape[1] // 2
    pieces = [lax.dynamic_index_in_dim(partial, me ^ k, 2, keepdims=False) for k in range(4)]
    low = [piece[:, :half] for piece in pieces]
    high = [piece[:, half:] for piece in pieces]
    return low[:3] + high[:3] + [swap(low[3], "dp", 1), swap(high[3], "dp", 2)]


def scatter_dp_second(items):
    if len(items) == 1:
        return items
    low = items[:3]
    high = items[3:6]
    low_two = (wide(low[2]) + wide(items[6])).astype(jnp.bfloat16)
    high_one = (wide(high[1]) + wide(items[7])).astype(jnp.bfloat16)
    return [low[0], high[0], swap(low[1], "dp", 1), swap(high[2], "dp", 2), low_two, high_one]


def scatter_dp_third(items):
    if len(items) == 1:
        return items[0]
    low, high, low_more, high_more, low_two, high_one = items
    low_sum = wide(low) + wide(low_more) + wide(swap(low_two, "dp", 2))
    high_sum = wide(high) + wide(high_more) + wide(swap(high_one, "dp", 1))
    return jnp.concatenate([low_sum, high_sum], 1).astype(jnp.bfloat16)


def to_columns(weight):
    seq_size = lax.axis_size("seq")
    slots, rows, width = weight.shape
    send = weight.reshape(slots, rows, seq_size, width // seq_size).transpose(2, 0, 1, 3)
    return lax.all_to_all(send, "seq", 0, 0).transpose(1, 0, 2, 3)


def to_rows(mine):
    return lax.all_to_all(mine.transpose(1, 0, 2, 3), "seq", 0, 0)


def after(value, *earlier):
    return lax.optimization_barrier((value,) + earlier)[0]


def to_rows_first(grads):
    seq_size = lax.axis_size("seq")
    dp_size = lax.axis_size("dp")
    partial = jnp.stack([grad.astype(jnp.bfloat16) for grad in grads], 0)
    slots, total, part = partial.shape
    rows = total // (seq_size * dp_size)
    return scatter_dp_first(partial.reshape(slots, seq_size, dp_size, rows, part))


def sum_all(value):
    for axis in ("seq", "dp"):
        offset = 1
        while offset < lax.axis_size(axis):
            value = value + swap(value, axis, offset)
            offset = offset * 2
    return value


def gather_tokens(local_rows):
    full = lax.all_gather(local_rows, "seq", axis=0)
    return full.reshape(-1, local_rows.shape[-1])


def scatter_tokens(partial, shape):
    send = partial.astype(jnp.bfloat16).reshape((lax.axis_size("seq"),) + shape)
    return lax.psum_scatter(send, "seq", scatter_dimension=0).astype(jnp.float32)


def local(
    tokens,
    segments,
    cotangent,
    attention_weight,
    attention_first,
    attention_second,
    feed_weight,
    feed_first,
    feed_second,
    gains,
    gains_first,
    gains_second,
    rel_table,
    table_first,
    table_second,
):
    micro_count, local_rows, width = tokens.shape
    shape = tokens.shape
    seq_size = lax.axis_size("seq")
    seq_len = local_rows * seq_size
    heads_here = HEADS // seq_size
    part = heads_here * HEAD_DIM
    seq_index = lax.axis_index("seq")

    attention_slots = attention_weight.transpose(1, 0, 2).astype(jnp.bfloat16)
    feed_slots = feed_weight.transpose(1, 0, 2).astype(jnp.bfloat16)
    inputs = tokens.astype(jnp.float32)
    normed_here = rms_norm(inputs, gains[0]).astype(jnp.bfloat16)
    attention_mine, normed_here = lax.optimization_barrier(
        (to_columns(attention_slots), normed_here)
    )
    normed_one = gather_tokens(normed_here)
    attention_items, late_cotangent = lax.optimization_barrier(
        (gather_dp_first(attention_mine), cotangent)
    )
    attention_low = gather_dp_second(attention_items)
    weight_out = attention_low[3]

    positions = jnp.arange(seq_len, dtype=jnp.int32)
    buckets = rel_bucket(positions[None, :] - positions[:, None])
    bucket_match = buckets[None, :, :] == jnp.arange(NUM_BUCKETS, dtype=jnp.int32)[:, None, None]
    table_here = lax.dynamic_slice_in_dim(rel_table, seq_index * heads_here, heads_here, 1)
    bias = jnp.einsum(
        "atj,ao->otj",
        bucket_match.astype(jnp.float32),
        table_here,
        precision=HIGHEST,
        preferred_element_type=jnp.float32,
    )

    def as_blocks(matrix):
        return matrix.astype(jnp.bfloat16).reshape(seq_size, micro_count, local_rows, part)

    grad_out = gather_tokens(late_cotangent)
    query, key, value = [
        as_blocks(dot(normed_one, attention_low[slot])) for slot in range(3)
    ]
    query, key, value, feed_slots = lax.optimization_barrier((query, key, value, feed_slots))
    feed_mine = to_columns(feed_slots)
    attended = attention_forward(query, key, value, bias, segments).reshape(-1, part)
    attention_partial, grad_out, feed_mine = lax.optimization_barrier(
        (dot_t(attended, weight_out).astype(jnp.bfloat16), grad_out, feed_mine)
    )
    feed_gathered = gather_dp_first(feed_mine)
    attention_out = scatter_tokens(attention_partial, shape)
    attention_out, feed_gathered = lax.optimization_barrier((attention_out, feed_gathered))
    feed_low = gather_dp_second(feed_gathered)
    weight_gate, weight_up, weight_down = feed_low[0], feed_low[1], feed_low[2]
    hidden_state = inputs + attention_out
    normed_two = gather_tokens(rms_norm(hidden_state, gains[1]).astype(jnp.bfloat16))
    grad_inner = dot(grad_out, weight_down)
    inner, grad_gate, grad_up, grad_two = feed_middle(
        normed_two, grad_inner, weight_gate, weight_up
    )
    feed_partial = dot_t(inner, weight_down).astype(jnp.bfloat16)
    grad_normed_two = scatter_tokens(grad_two, shape)
    grads_feed = [
        outer_sum(normed_two, grad_gate).astype(jnp.bfloat16),
        outer_sum(normed_two, grad_up).astype(jnp.bfloat16),
        outer_sum(grad_out, inner).astype(jnp.bfloat16),
    ]
    feed_steps = to_rows_first(grads_feed)
    grad_normed_two, feed_steps, feed_partial = lax.optimization_barrier(
        (grad_normed_two, feed_steps, feed_partial)
    )
    feed_steps = scatter_dp_second(feed_steps)
    grad_hidden_norm, grad_gain_two = norm_back(hidden_state, gains[1], grad_normed_two)
    grad_hidden = cotangent.astype(jnp.float32) + grad_hidden_norm
    grad_branch = gather_tokens(grad_hidden.astype(jnp.bfloat16))
    grad_branch, feed_mine_grad = lax.optimization_barrier(
        (grad_branch, scatter_dp_third(feed_steps))
    )
    grad_attended = as_blocks(dot(grad_branch, weight_out))
    feed_total = to_rows(feed_mine_grad)
    grad_query, grad_key, grad_value, score_sums = attention_backward(
        query, key, value, grad_attended, bias, segments
    )
    grad_table_here = jnp.einsum(
        "hij,zij->zh",
        score_sums.astype(jnp.bfloat16),
        bucket_match.astype(jnp.bfloat16),
        preferred_element_type=jnp.float32,
    )
    grad_qkv = [item.reshape(-1, part) for item in (grad_query, grad_key, grad_value)]
    normed_partial = sum(dot_t(grad_qkv[slot], attention_low[slot]) for slot in range(3))
    normed_partial, feed_total = lax.optimization_barrier(
        (normed_partial.astype(jnp.bfloat16), feed_total)
    )
    grad_normed_one = scatter_tokens(normed_partial, shape)
    block_rows = hidden_state + scatter_tokens(after(feed_partial, grad_normed_one), shape)
    block_rows = block_rows.astype(jnp.bfloat16)
    attention_steps = to_rows_first(
        [outer_sum(normed_one, item) for item in grad_qkv] + [outer_sum(grad_branch, attended)]
    )
    attention_total = to_rows(scatter_dp_third(scatter_dp_second(attention_steps)))
    grad_input_norm, grad_gain_one = norm_back(inputs, gains[0], grad_normed_one)
    grad_rows = (grad_hidden + grad_input_norm).astype(jnp.bfloat16)
    grad_table = lax.dynamic_update_slice_in_dim(
        jnp.zeros((NUM_BUCKETS, HEADS), jnp.float32), grad_table_here, seq_index * heads_here, 1
    )
    new_feed = update_feed(feed_weight, feed_first, feed_second, feed_total)
    small = jnp.concatenate([grad_gain_one, grad_gain_two, grad_table.reshape(-1)])
    small, new_feed = lax.optimization_barrier((small, new_feed))
    small = sum_all(small.reshape(-1, 128)).reshape(-1)
    gains_total = small[: 2 * width].reshape(2, width)
    table_total = small[2 * width :].reshape(NUM_BUCKETS, HEADS)
    new_attention = update_attention(
        attention_weight, attention_first, attention_second, attention_total
    )
    new_gains = adam_update(gains, gains_first, gains_second, gains_total, 0.6, 0.0)
    new_table = adam_update(rel_table, table_first, table_second, table_total, 1.5, 0.0)
    return (
        block_rows,
        grad_rows,
        new_attention[0],
        new_attention[1],
        new_attention[2],
        new_attention[3],
        new_feed[0],
        new_feed[1],
        new_feed[2],
        new_gains[0],
        new_gains[1],
        new_gains[2],
        new_table[0],
        new_table[1],
        new_table[2],
    )


def solution(mesh):
    in_specs = (
        P("dp", "seq", None),
        P("dp", None),
        P("dp", "seq", None),
        P(("seq", "dp"), None, None),
        P(("seq", "dp"), None, None),
        P(("seq", "dp"), None, None),
        P(("seq", "dp"), None, None),
        P(("seq", "dp"), None, None),
        P(("seq", "dp"), None, None),
        P(),
        P(),
        P(),
        P(),
        P(),
        P(),
    )
    out_specs = (
        P("dp", "seq", None),
        P("dp", "seq", None),
        P(("seq", "dp"), None, None),
        P(("seq", "dp"), None, None),
        P(("seq", "dp"), None, None),
        P(("seq", "dp"), None),
        P(("seq", "dp"), None, None),
        P(("seq", "dp"), None, None),
        P(("seq", "dp"), None, None),
        P(),
        P(),
        P(),
        P(),
        P(),
        P(),
    )
    return jax.shard_map(local, mesh=mesh, in_specs=in_specs, out_specs=out_specs, check_vma=False)
```

```python
import math

import jax
import jax.numpy as jnp
from jax import lax
from jax.experimental import pallas as pl
from jax.experimental.pallas import tpu as pltpu
from jax.sharding import PartitionSpec as P

D = 2048
HEADS = 32
HEAD_DIM = 64
FF = 5120
NUM_BUCKETS = 32
MAX_DIST = 128
STEP = 10


NORM_EPSILON = 1e-06
NEG_BIG = -1000000000.0
BETA_ONE = 0.9
BETA_TWO = 0.95
EPS_ADAM = 1e-08
DECAY = 0.1
HIGHEST = lax.Precision.HIGHEST


def rms_norm(values, gain_vec):
    inv_root = lax.rsqrt(jnp.mean(values * values, axis=-1, keepdims=True) + NORM_EPSILON)
    return values * inv_root * gain_vec


def bucket_edges():
    half_count = NUM_BUCKETS // 2
    exact_count = half_count // 2
    log_count = half_count - exact_count
    far_ratio = MAX_DIST // exact_count
    edge_list = []
    for step_index in range(1, log_count):
        edge_at = exact_count
        while edge_at**log_count < exact_count**log_count * far_ratio**step_index:
            edge_at = edge_at + 1
        edge_list.append(edge_at)
    return edge_list


def rel_bucket(relative):
    half_count = NUM_BUCKETS // 2
    exact_count = half_count // 2
    distance = jnp.abs(relative)
    far_bucket = jnp.full(relative.shape, exact_count, jnp.int32)
    for edge_at in bucket_edges():
        far_bucket = far_bucket + (distance >= edge_at).astype(jnp.int32)
    near_far = jnp.where(distance < exact_count, distance, far_bucket)
    return near_far + jnp.where(relative > 0, half_count, 0)


def adam_update(weight, first, second, grads, rate, decay):
    first_new = BETA_ONE * first + (1.0 - BETA_ONE) * grads
    second_new = BETA_TWO * second + (1.0 - BETA_TWO) * grads * grads
    first_hat = first_new / (1.0 - BETA_ONE**STEP)
    second_hat = second_new / (1.0 - BETA_TWO**STEP)
    weight_new = weight - rate * (first_hat / (jnp.sqrt(second_hat) + EPS_ADAM) + decay * weight)
    return (weight_new, first_new, second_new)


def attention_rates():
    return 3.0 * jnp.array(
        [D ** (-0.5), (32 * D) ** (-0.5), D ** (-0.5), (HEADS * HEAD_DIM // 64) ** (-0.5)],
        jnp.float32,
    ).reshape(1, 4, 1)


def feed_rates():
    return 3.0 * jnp.array([D ** (-0.5), D ** (-0.5), FF ** (-0.5)], jnp.float32).reshape(1, 3, 1)


def dot(left, right):
    return jnp.dot(left, right, preferred_element_type=jnp.float32)


def dot_t(left, right):
    return lax.dot_general(
        left, right, (((1,), (1,)), ((), ())), preferred_element_type=jnp.float32
    )


def outer_sum(left, right):
    return lax.dot_general(
        left, right, (((0,), (0,)), ((), ())), preferred_element_type=jnp.float32
    )


def norm_stats(values):
    return lax.rsqrt(jnp.mean(values * values, axis=-1, keepdims=True) + NORM_EPSILON)


def norm_back(values, gain_vec, grads):
    inv_root = norm_stats(values)
    unit = values * inv_root
    scaled = grads * gain_vec
    grad_in = inv_root * (scaled - unit * jnp.mean(unit * scaled, axis=-1, keepdims=True))
    return grad_in, jnp.sum(grads * unit, axis=(0, 1))


def feed_middle(normed, grad_inner, weight_gate, weight_up):
    tokens, width = normed.shape
    hidden = weight_gate.shape[1]
    block = min(512, tokens)
    scale = (2.0 / math.pi) ** 0.5

    def body(n_ref, gi_ref, wg_ref, wu_ref, inner_ref, gg_ref, gu_ref, out_ref):
        gate = dot(n_ref[...], wg_ref[...])
        up = dot(n_ref[...], wu_ref[...])
        grad_inner = gi_ref[...]
        squared = gate * gate
        tanh = jnp.tanh(scale * (gate + 0.044715 * (squared * gate)))
        half = 0.5 * (1.0 + tanh)
        act = gate * half
        slope = half + 0.5 * gate * (1.0 - tanh * tanh) * (scale * (1.0 + 0.134145 * squared))
        inner_ref[...] = (act * up).astype(jnp.bfloat16)
        grad_gate = (grad_inner * up * slope).astype(jnp.bfloat16)
        grad_up = (grad_inner * act).astype(jnp.bfloat16)
        gg_ref[...] = grad_gate
        gu_ref[...] = grad_up
        total = dot_t(grad_gate, wg_ref[...]) + dot_t(grad_up, wu_ref[...])
        out_ref[...] = total.astype(jnp.bfloat16)

    rows = pl.BlockSpec((block, width), lambda i: (i, 0))
    units = pl.BlockSpec((block, hidden), lambda i: (i, 0))
    weights = pl.BlockSpec((width, hidden), lambda i: (0, 0))
    low_units = jax.ShapeDtypeStruct((tokens, hidden), jnp.bfloat16)
    return pl.pallas_call(
        body,
        grid=(tokens // block,),
        in_specs=[rows, units, weights, weights],
        out_specs=[units, units, units, rows],
        out_shape=[
            low_units,
            low_units,
            low_units,
            jax.ShapeDtypeStruct((tokens, width), jnp.bfloat16),
        ],
        compiler_params=pltpu.CompilerParams(vmem_limit_bytes=56 * MIB),
        cost_estimate=pl.CostEstimate(
            flops=8 * tokens * width * hidden,
            bytes_accessed=4 * tokens * width + 10 * tokens * hidden + 4 * width * hidden,
            transcendentals=tokens * hidden,
        ),
    )(normed, grad_inner, weight_gate, weight_up)


def partner_pairs(axis, offset):
    return [(index, index ^ offset) for index in range(lax.axis_size(axis))]


def swap(value, axis, offset):
    return lax.ppermute(value, axis, partner_pairs(axis, offset))


MIB = 1024 * 1024
ADAM_PARAMS = pltpu.CompilerParams(vmem_limit_bytes=32 * MIB)


def attention_params(length):
    return pltpu.CompilerParams(vmem_limit_bytes=min(56, length * length // 8192) * MIB)


def adam_values(weight, first, second, grads, rate, decay):
    first_new = BETA_ONE * first + (1.0 - BETA_ONE) * grads
    second_new = BETA_TWO * second + (1.0 - BETA_TWO) * grads * grads
    first_hat = first_new * (1.0 / (1.0 - BETA_ONE**STEP))
    root = jnp.sqrt(second_new * (1.0 / (1.0 - BETA_TWO**STEP)))
    weight_new = weight - rate * (first_hat / (root + EPS_ADAM) + decay * weight)
    return (weight_new, first_new, second_new)


def in_columns(grads):
    seq_size, slots, rows, part = grads.shape
    return wide(grads).transpose(2, 1, 0, 3).reshape(rows, slots, seq_size * part)


def update_attention(weight, first, second, grads):
    seq_size, slots, rows, part = grads.shape
    width = seq_size * part
    if part % 128:
        new = adam_update(weight, first, second, in_columns(grads), attention_rates(), DECAY)
        return new[0], new[1], new[2][:, :3], new[2][:, 3]
    chunk = 2
    scales = [D ** (-0.5), (32 * D) ** (-0.5), D ** (-0.5), (HEADS * HEAD_DIM // 64) ** (-0.5)]

    def body(w_ref, m_ref, v_ref, g_ref, w_out, m_out, v_out, o_out):
        for slot in range(slots):
            for item in range(chunk):
                cols = slice(item * part, (item + 1) * part)
                new = adam_values(
                    w_ref[:, slot, cols],
                    m_ref[:, slot, cols],
                    v_ref[:, slot, cols],
                    wide(g_ref[item, slot]),
                    3.0 * scales[slot],
                    DECAY,
                )
                w_out[:, slot, cols] = new[0]
                m_out[:, slot, cols] = new[1]
                if slot < slots - 1:
                    v_out[slot, :, cols] = new[2]
                else:
                    o_out[:, cols] = new[2]

    state_spec = pl.BlockSpec((rows, slots, chunk * part), lambda j: (0, 0, j))
    new = pl.pallas_call(
        body,
        grid=(seq_size // chunk,),
        in_specs=[state_spec] * 3
        + [pl.BlockSpec((chunk, slots, rows, part), lambda j: (j, 0, 0, 0))],
        out_specs=[
            state_spec,
            state_spec,
            pl.BlockSpec((slots - 1, rows, chunk * part), lambda j: (0, 0, j)),
            pl.BlockSpec((rows, chunk * part), lambda j: (0, j)),
        ],
        out_shape=[
            jax.ShapeDtypeStruct(weight.shape, jnp.float32),
            jax.ShapeDtypeStruct(weight.shape, jnp.float32),
            jax.ShapeDtypeStruct((slots - 1, rows, width), jnp.float32),
            jax.ShapeDtypeStruct((rows, width), jnp.float32),
        ],
        compiler_params=ADAM_PARAMS,
        cost_estimate=pl.CostEstimate(
            flops=20 * weight.size, bytes_accessed=26 * weight.size, transcendentals=weight.size
        ),
    )(weight, first, second, grads)
    return new[0], new[1], new[2].transpose(1, 0, 2), new[3]


def update_feed(weight, first, second, grads):
    seq_size, slots, rows, part = grads.shape
    if part % 128:
        return adam_update(weight, first, second, in_columns(grads), feed_rates(), DECAY)

    def body(w_ref, m_ref, v_ref, g_ref, w_out, m_out, v_out):
        rate = jnp.where(pl.program_id(0) == slots - 1, 3.0 * FF ** (-0.5), 3.0 * D ** (-0.5))
        for item in range(chunk):
            cols = slice(item * part, (item + 1) * part)
            new = adam_values(
                w_ref[0, :, cols],
                m_ref[0, :, cols],
                v_ref[0, :, cols],
                wide(g_ref[item, 0]),
                rate,
                DECAY,
            )
            for ref, value in zip((w_out, m_out, v_out), new):
                ref[0, :, cols] = value

    chunk = 4
    state_spec = pl.BlockSpec((1, rows, chunk * part), lambda slot, j: (slot, 0, j))
    state = [item.transpose(1, 0, 2) for item in (weight, first, second)]
    new = pl.pallas_call(
        body,
        grid=(slots, seq_size // chunk),
        in_specs=[state_spec] * 3
        + [pl.BlockSpec((chunk, 1, rows, part), lambda slot, j: (j, slot, 0, 0))],
        out_specs=[state_spec] * 3,
        out_shape=[jax.ShapeDtypeStruct(state[0].shape, jnp.float32)] * 3,
        compiler_params=ADAM_PARAMS,
        cost_estimate=pl.CostEstimate(
            flops=20 * weight.size, bytes_accessed=26 * weight.size, transcendentals=weight.size
        ),
    )(*state, grads)
    return [item.transpose(1, 0, 2) for item in new]


def head_probs(query, key, bias, same_doc):
    scores = lax.dot_general(
        query, key, (((1,), (1,)), ((), ())), preferred_element_type=jnp.float32
    )
    scores = jnp.where(same_doc, scores + bias, NEG_BIG)
    exp_scores = jnp.exp(scores - jnp.max(scores, axis=-1, keepdims=True))
    return exp_scores * (1.0 / jnp.sum(exp_scores, axis=-1, keepdims=True))


def attention_specs(seq_size, rows):
    length = seq_size * rows
    tokens_spec = pl.BlockSpec((seq_size, 1, rows, 128), lambda pair, m: (0, m, 0, pair))
    return tokens_spec, [
        pl.BlockSpec((2, length, length), lambda pair, m: (pair, 0, 0)),
        pl.BlockSpec((1, length, 1), lambda pair, m: (m, 0, 0)),
        pl.BlockSpec((1, 1, length), lambda pair, m: (m, 0, 0)),
    ]


def attention_forward(query, key, value, bias, segments):
    seq_size, micro_count, rows, part = query.shape
    length = seq_size * rows
    tokens_spec, other_specs = attention_specs(seq_size, rows)

    def body(q_ref, k_ref, v_ref, bias_ref, seg_q_ref, seg_k_ref, out_ref):
        q, k, v = [ref[:, 0].reshape(length, 128) for ref in (q_ref, k_ref, v_ref)]
        same_doc = seg_q_ref[0] == seg_k_ref[0]
        outs = []
        for h in range(2):
            cols = slice(h * HEAD_DIM, (h + 1) * HEAD_DIM)
            probs = head_probs(q[:, cols], k[:, cols], bias_ref[h], same_doc)
            outs.append(dot(probs.astype(jnp.bfloat16), v[:, cols]))
        out = jnp.concatenate(outs, 1).astype(jnp.bfloat16)
        out_ref[...] = out.reshape(seq_size, 1, rows, 128)

    return pl.pallas_call(
        body,
        grid=(part // 128, micro_count),
        in_specs=[tokens_spec] * 3 + other_specs,
        out_specs=tokens_spec,
        out_shape=jax.ShapeDtypeStruct(query.shape, jnp.bfloat16),
        compiler_params=attention_params(length),
        cost_estimate=pl.CostEstimate(
            flops=6000 * length * query.size // HEAD_DIM,
            bytes_accessed=8 * query.size + bias.size * 4,
            transcendentals=length * query.size // HEAD_DIM,
        ),
    )(query, key, value, bias, segments[:, :, None], segments[:, None, :])


def attention_backward(query, key, value, grad_out, bias, segments):
    seq_size, micro_count, rows, part = query.shape
    length = seq_size * rows
    tokens_spec, other_specs = attention_specs(seq_size, rows)

    def body(
        q_ref, k_ref, v_ref, g_ref, bias_ref, seg_q_ref, seg_k_ref, dq_ref, dk_ref, dv_ref, ds_ref
    ):
        q, k, v, g = [ref[:, 0].reshape(length, 128) for ref in (q_ref, k_ref, v_ref, g_ref)]
        same_doc = seg_q_ref[0] == seg_k_ref[0]
        first = pl.program_id(1) == 0
        grads = ([], [], [])
        for h in range(2):
            cols = slice(h * HEAD_DIM, (h + 1) * HEAD_DIM)
            probs = head_probs(q[:, cols], k[:, cols], bias_ref[h], same_doc)
            grad_probs = dot_t(g[:, cols], v[:, cols])
            row_dot = jnp.sum(probs * grad_probs, axis=-1, keepdims=True)
            grad_scores = (probs * (grad_probs - row_dot)).astype(jnp.bfloat16)
            wide = grad_scores.astype(jnp.float32)
            ds_ref[h] = jnp.where(first, wide, ds_ref[h] + wide)
            grads[0].append(dot(grad_scores, k[:, cols]))
            grads[1].append(outer_sum(grad_scores, q[:, cols]))
            grads[2].append(outer_sum(probs.astype(jnp.bfloat16), g[:, cols]))
        for ref, parts in zip((dq_ref, dk_ref, dv_ref), grads):
            joined = jnp.concatenate(parts, 1).astype(jnp.bfloat16)
            ref[...] = joined.reshape(seq_size, 1, rows, 128)

    return pl.pallas_call(
        body,
        grid=(part // 128, micro_count),
        in_specs=[tokens_spec] * 4 + other_specs,
        out_specs=[tokens_spec] * 3
        + [pl.BlockSpec((2, length, length), lambda pair, m: (pair, 0, 0))],
        out_shape=[jax.ShapeDtypeStruct(query.shape, jnp.bfloat16)] * 3
        + [jax.ShapeDtypeStruct((part // HEAD_DIM, length, length), jnp.float32)],
        compiler_params=attention_params(length),
        cost_estimate=pl.CostEstimate(
            flops=8000 * length * query.size // HEAD_DIM,
            bytes_accessed=14 * query.size + bias.size * 8,
            transcendentals=length * query.size // HEAD_DIM,
        ),
    )(query, key, value, grad_out, bias, segments[:, :, None], segments[:, None, :])


def gather_dp_first(mine):
    if lax.axis_size("dp") != 4:
        return [lax.all_gather(mine, "dp", axis=2)]
    return [mine, swap(mine, "dp", 1), swap(mine, "dp", 2)]


def gather_dp_second(items):
    if len(items) == 1:
        full = items[0]
    else:
        mine, one, two = items
        me = lax.axis_index("dp")
        half = mine.shape[1] // 2
        low = swap(one[:, :half], "dp", 2)
        high = swap(two[:, half:], "dp", 1)
        full = jnp.zeros(mine.shape[:2] + (4,) + mine.shape[2:], mine.dtype)
        for piece, source, start in (
            (mine, 0, 0),
            (one, 1, 0),
            (two, 2, 0),
            (low, 3, 0),
            (high, 3, half),
        ):
            full = lax.dynamic_update_slice(full, piece[:, :, None], (0, start, me ^ source, 0, 0))
    return full.reshape(full.shape[0], -1, full.shape[-1])


def wide(value):
    return value.astype(jnp.float32)


def scatter_dp_first(partial):
    if lax.axis_size("dp") != 4:
        return [lax.psum_scatter(partial, "dp", scatter_dimension=2)]
    me = lax.axis_index("dp")
    half = partial.shape[1] // 2
    pieces = [lax.dynamic_index_in_dim(partial, me ^ k, 2, keepdims=False) for k in range(4)]
    low = [piece[:, :half] for piece in pieces]
    high = [piece[:, half:] for piece in pieces]
    return low[:3] + high[:3] + [swap(low[3], "dp", 1), swap(high[3], "dp", 2)]


def scatter_dp_second(items):
    if len(items) == 1:
        return items
    low = items[:3]
    high = items[3:6]
    low_two = (wide(low[2]) + wide(items[6])).astype(jnp.bfloat16)
    high_one = (wide(high[1]) + wide(items[7])).astype(jnp.bfloat16)
    return [low[0], high[0], swap(low[1], "dp", 1), swap(high[2], "dp", 2), low_two, high_one]


def scatter_dp_third(items):
    if len(items) == 1:
        return items[0]
    low, high, low_more, high_more, low_two, high_one = items
    low_sum = wide(low) + wide(low_more) + wide(swap(low_two, "dp", 2))
    high_sum = wide(high) + wide(high_more) + wide(swap(high_one, "dp", 1))
    return jnp.concatenate([low_sum, high_sum], 1).astype(jnp.bfloat16)


def to_columns(weight):
    seq_size = lax.axis_size("seq")
    slots, rows, width = weight.shape
    send = weight.reshape(slots, rows, seq_size, width // seq_size).transpose(2, 0, 1, 3)
    return lax.all_to_all(send, "seq", 0, 0).transpose(1, 0, 2, 3)


def to_rows(mine):
    return lax.all_to_all(mine.transpose(1, 0, 2, 3), "seq", 0, 0)


def after(value, *earlier):
    return lax.optimization_barrier((value,) + earlier)[0]


def to_rows_first(grads):
    seq_size = lax.axis_size("seq")
    dp_size = lax.axis_size("dp")
    partial = jnp.stack([grad.astype(jnp.bfloat16) for grad in grads], 0)
    slots, total, part = partial.shape
    rows = total // (seq_size * dp_size)
    return scatter_dp_first(partial.reshape(slots, seq_size, dp_size, rows, part))


def sum_all(value):
    for axis in ("seq", "dp"):
        offset = 1
        while offset < lax.axis_size(axis):
            value = value + swap(value, axis, offset)
            offset = offset * 2
    return value


def gather_tokens(local_rows):
    full = lax.all_gather(local_rows, "seq", axis=0)
    return full.reshape(-1, local_rows.shape[-1])


def scatter_tokens(partial, shape):
    send = partial.astype(jnp.bfloat16).reshape((lax.axis_size("seq"),) + shape)
    return lax.psum_scatter(send, "seq", scatter_dimension=0).astype(jnp.float32)


def local(
    tokens,
    segments,
    cotangent,
    attention_weight,
    attention_first,
    attention_second,
    feed_weight,
    feed_first,
    feed_second,
    gains,
    gains_first,
    gains_second,
    rel_table,
    table_first,
    table_second,
):
    micro_count, local_rows, width = tokens.shape
    shape = tokens.shape
    seq_size = lax.axis_size("seq")
    seq_len = local_rows * seq_size
    heads_here = HEADS // seq_size
    part = heads_here * HEAD_DIM
    seq_index = lax.axis_index("seq")

    attention_slots = attention_weight.transpose(1, 0, 2).astype(jnp.bfloat16)
    feed_slots = feed_weight.transpose(1, 0, 2).astype(jnp.bfloat16)
    inputs = tokens.astype(jnp.float32)
    normed_here = rms_norm(inputs, gains[0]).astype(jnp.bfloat16)
    attention_mine, normed_here = lax.optimization_barrier(
        (to_columns(attention_slots), normed_here)
    )
    normed_one = gather_tokens(normed_here)
    attention_items, late_cotangent = lax.optimization_barrier(
        (gather_dp_first(attention_mine), cotangent)
    )
    attention_low = gather_dp_second(attention_items)
    weight_out = attention_low[3]

    positions = jnp.arange(seq_len, dtype=jnp.int32)
    buckets = rel_bucket(positions[None, :] - positions[:, None])
    bucket_match = buckets[None, :, :] == jnp.arange(NUM_BUCKETS, dtype=jnp.int32)[:, None, None]
    table_here = lax.dynamic_slice_in_dim(rel_table, seq_index * heads_here, heads_here, 1)
    bias = jnp.einsum(
        "atj,ao->otj",
        bucket_match.astype(jnp.float32),
        table_here,
        precision=HIGHEST,
        preferred_element_type=jnp.float32,
    )

    def as_blocks(matrix):
        return matrix.astype(jnp.bfloat16).reshape(seq_size, micro_count, local_rows, part)

    grad_out = gather_tokens(late_cotangent)
    query, key, value = [
        as_blocks(dot(normed_one, attention_low[slot])) for slot in range(3)
    ]
    query, key, value, feed_slots = lax.optimization_barrier((query, key, value, feed_slots))
    feed_mine = to_columns(feed_slots)
    attended = attention_forward(query, key, value, bias, segments).reshape(-1, part)
    attention_partial, grad_out, feed_mine = lax.optimization_barrier(
        (dot_t(attended, weight_out).astype(jnp.bfloat16), grad_out, feed_mine)
    )
    feed_gathered = gather_dp_first(feed_mine)
    attention_out = scatter_tokens(attention_partial, shape)
    attention_out, feed_gathered = lax.optimization_barrier((attention_out, feed_gathered))
    feed_low = gather_dp_second(feed_gathered)
    weight_gate, weight_up, weight_down = feed_low[0], feed_low[1], feed_low[2]
    hidden_state = inputs + attention_out
    normed_two = gather_tokens(rms_norm(hidden_state, gains[1]).astype(jnp.bfloat16))
    grad_inner = dot(grad_out, weight_down)
    inner, grad_gate, grad_up, grad_two = feed_middle(
        normed_two, grad_inner, weight_gate, weight_up
    )
    feed_partial = dot_t(inner, weight_down).astype(jnp.bfloat16)
    grad_normed_two = scatter_tokens(grad_two, shape)
    grads_feed = [
        outer_sum(normed_two, grad_gate).astype(jnp.bfloat16),
        outer_sum(normed_two, grad_up).astype(jnp.bfloat16),
        outer_sum(grad_out, inner).astype(jnp.bfloat16),
    ]
    feed_steps = to_rows_first(grads_feed)
    grad_normed_two, feed_steps, feed_partial = lax.optimization_barrier(
        (grad_normed_two, feed_steps, feed_partial)
    )
    feed_steps = scatter_dp_second(feed_steps)
    grad_hidden_norm, grad_gain_two = norm_back(hidden_state, gains[1], grad_normed_two)
    grad_hidden = cotangent.astype(jnp.float32) + grad_hidden_norm
    grad_branch = gather_tokens(grad_hidden.astype(jnp.bfloat16))
    grad_branch, feed_mine_grad = lax.optimization_barrier(
        (grad_branch, scatter_dp_third(feed_steps))
    )
    grad_attended = as_blocks(dot(grad_branch, weight_out))
    feed_total = to_rows(feed_mine_grad)
    grad_query, grad_key, grad_value, score_sums = attention_backward(
        query, key, value, grad_attended, bias, segments
    )
    grad_table_here = jnp.einsum(
        "hij,zij->zh",
        score_sums.astype(jnp.bfloat16),
        bucket_match.astype(jnp.bfloat16),
        preferred_element_type=jnp.float32,
    )
    grad_qkv = [item.reshape(-1, part) for item in (grad_query, grad_key, grad_value)]
    normed_partial = sum(dot_t(grad_qkv[slot], attention_low[slot]) for slot in range(3))
    normed_partial, feed_total = lax.optimization_barrier(
        (normed_partial.astype(jnp.bfloat16), feed_total)
    )
    grad_normed_one = scatter_tokens(normed_partial, shape)
    block_rows = hidden_state + scatter_tokens(after(feed_partial, grad_normed_one), shape)
    block_rows = block_rows.astype(jnp.bfloat16)
    attention_steps = to_rows_first(
        [outer_sum(normed_one, item) for item in grad_qkv] + [outer_sum(grad_branch, attended)]
    )
    attention_total = to_rows(scatter_dp_third(scatter_dp_second(attention_steps)))
    grad_input_norm, grad_gain_one = norm_back(inputs, gains[0], grad_normed_one)
    grad_rows = (grad_hidden + grad_input_norm).astype(jnp.bfloat16)
    grad_table = lax.dynamic_update_slice_in_dim(
        jnp.zeros((NUM_BUCKETS, HEADS), jnp.float32), grad_table_here, seq_index * heads_here, 1
    )
    new_feed = update_feed(feed_weight, feed_first, feed_second, feed_total)
    small = jnp.concatenate([grad_gain_one, grad_gain_two, grad_table.reshape(-1)])
    small, new_feed = lax.optimization_barrier((small, new_feed))
    small = sum_all(small.reshape(-1, 128)).reshape(-1)
    gains_total = small[: 2 * width].reshape(2, width)
    table_total = small[2 * width :].reshape(NUM_BUCKETS, HEADS)
    new_attention = update_attention(
        attention_weight, attention_first, attention_second, attention_total
    )
    new_gains = adam_update(gains, gains_first, gains_second, gains_total, 0.6, 0.0)
    new_table = adam_update(rel_table, table_first, table_second, table_total, 1.5, 0.0)
    return (
        block_rows,
        grad_rows,
        new_attention[0],
        new_attention[1],
        new_attention[2],
        new_attention[3],
        new_feed[0],
        new_feed[1],
        new_feed[2],
        new_gains[0],
        new_gains[1],
        new_gains[2],
        new_table[0],
        new_table[1],
        new_table[2],
    )


def solution(mesh):
    in_specs = (
        P("dp", "seq", None),
        P("dp", None),
        P("dp", "seq", None),
        P(("seq", "dp"), None, None),
        P(("seq", "dp"), None, None),
        P(("seq", "dp"), None, None),
        P(("seq", "dp"), None, None),
        P(("seq", "dp"), None, None),
        P(("seq", "dp"), None, None),
        P(),
        P(),
        P(),
        P(),
        P(),
        P(),
    )
    out_specs = (
        P("dp", "seq", None),
        P("dp", "seq", None),
        P(("seq", "dp"), None, None),
        P(("seq", "dp"), None, None),
        P(("seq", "dp"), None, None),
        P(("seq", "dp"), None),
        P(("seq", "dp"), None, None),
        P(("seq", "dp"), None, None),
        P(("seq", "dp"), None, None),
        P(),
        P(),
        P(),
        P(),
        P(),
        P(),
    )
    return jax.shard_map(local, mesh=mesh, in_specs=in_specs, out_specs=out_specs, check_vma=False)
```

```python
import math

import jax
import jax.numpy as jnp
from jax import lax
from jax.experimental import pallas as pl
from jax.experimental.pallas import tpu as pltpu
from jax.sharding import PartitionSpec as P

D = 2048
HEADS = 32
HEAD_DIM = 64
FF = 5120
NUM_BUCKETS = 32
MAX_DIST = 128
STEP = 10


NORM_EPSILON = 1e-06
NEG_BIG = -1000000000.0
BETA_ONE = 0.9
BETA_TWO = 0.95
EPS_ADAM = 1e-08
DECAY = 0.1
HIGHEST = lax.Precision.HIGHEST


def rms_norm(values, gain_vec):
    inv_root = lax.rsqrt(jnp.mean(values * values, axis=-1, keepdims=True) + NORM_EPSILON)
    return values * inv_root * gain_vec


def bucket_edges():
    half_count = NUM_BUCKETS // 2
    exact_count = half_count // 2
    log_count = half_count - exact_count
    far_ratio = MAX_DIST // exact_count
    edge_list = []
    for step_index in range(1, log_count):
        edge_at = exact_count
        while edge_at**log_count < exact_count**log_count * far_ratio**step_index:
            edge_at = edge_at + 1
        edge_list.append(edge_at)
    return edge_list


def rel_bucket(relative):
    half_count = NUM_BUCKETS // 2
    exact_count = half_count // 2
    distance = jnp.abs(relative)
    far_bucket = jnp.full(relative.shape, exact_count, jnp.int32)
    for edge_at in bucket_edges():
        far_bucket = far_bucket + (distance >= edge_at).astype(jnp.int32)
    near_far = jnp.where(distance < exact_count, distance, far_bucket)
    return near_far + jnp.where(relative > 0, half_count, 0)


def adam_update(weight, first, second, grads, rate, decay):
    first_new = BETA_ONE * first + (1.0 - BETA_ONE) * grads
    second_new = BETA_TWO * second + (1.0 - BETA_TWO) * grads * grads
    first_hat = first_new / (1.0 - BETA_ONE**STEP)
    second_hat = second_new / (1.0 - BETA_TWO**STEP)
    weight_new = weight - rate * (first_hat / (jnp.sqrt(second_hat) + EPS_ADAM) + decay * weight)
    return (weight_new, first_new, second_new)


def attention_rates():
    return 3.0 * jnp.array(
        [D ** (-0.5), (32 * D) ** (-0.5), D ** (-0.5), (HEADS * HEAD_DIM // 64) ** (-0.5)],
        jnp.float32,
    ).reshape(1, 4, 1)


def feed_rates():
    return 3.0 * jnp.array([D ** (-0.5), D ** (-0.5), FF ** (-0.5)], jnp.float32).reshape(1, 3, 1)


def dot(left, right):
    return jnp.dot(left, right, preferred_element_type=jnp.float32)


def dot_t(left, right):
    return lax.dot_general(
        left, right, (((1,), (1,)), ((), ())), preferred_element_type=jnp.float32
    )


def outer_sum(left, right):
    return lax.dot_general(
        left, right, (((0,), (0,)), ((), ())), preferred_element_type=jnp.float32
    )


def norm_stats(values):
    return lax.rsqrt(jnp.mean(values * values, axis=-1, keepdims=True) + NORM_EPSILON)


def norm_back(values, gain_vec, grads):
    inv_root = norm_stats(values)
    unit = values * inv_root
    scaled = grads * gain_vec
    grad_in = inv_root * (scaled - unit * jnp.mean(unit * scaled, axis=-1, keepdims=True))
    return grad_in, jnp.sum(grads * unit, axis=(0, 1))


def feed_middle(normed, grad_inner, weight_gate, weight_up):
    tokens, width = normed.shape
    hidden = weight_gate.shape[1]
    block = min(512, tokens)
    scale = (2.0 / math.pi) ** 0.5

    def body(n_ref, gi_ref, wg_ref, wu_ref, inner_ref, gg_ref, gu_ref, out_ref):
        gate = dot(n_ref[...], wg_ref[...])
        up = dot(n_ref[...], wu_ref[...])
        grad_inner = gi_ref[...]
        squared = gate * gate
        tanh = jnp.tanh(scale * (gate + 0.044715 * (squared * gate)))
        half = 0.5 * (1.0 + tanh)
        act = gate * half
        slope = half + 0.5 * gate * (1.0 - tanh * tanh) * (scale * (1.0 + 0.134145 * squared))
        inner_ref[...] = (act * up).astype(jnp.bfloat16)
        grad_gate = (grad_inner * up * slope).astype(jnp.bfloat16)
        grad_up = (grad_inner * act).astype(jnp.bfloat16)
        gg_ref[...] = grad_gate
        gu_ref[...] = grad_up
        total = dot_t(grad_gate, wg_ref[...]) + dot_t(grad_up, wu_ref[...])
        out_ref[...] = total.astype(jnp.bfloat16)

    rows = pl.BlockSpec((block, width), lambda i: (i, 0))
    units = pl.BlockSpec((block, hidden), lambda i: (i, 0))
    weights = pl.BlockSpec((width, hidden), lambda i: (0, 0))
    low_units = jax.ShapeDtypeStruct((tokens, hidden), jnp.bfloat16)
    return pl.pallas_call(
        body,
        grid=(tokens // block,),
        in_specs=[rows, units, weights, weights],
        out_specs=[units, units, units, rows],
        out_shape=[
            low_units,
            low_units,
            low_units,
            jax.ShapeDtypeStruct((tokens, width), jnp.bfloat16),
        ],
        compiler_params=pltpu.CompilerParams(vmem_limit_bytes=56 * MIB),
        cost_estimate=pl.CostEstimate(
            flops=8 * tokens * width * hidden,
            bytes_accessed=4 * tokens * width + 10 * tokens * hidden + 4 * width * hidden,
            transcendentals=tokens * hidden,
        ),
    )(normed, grad_inner, weight_gate, weight_up)


def partner_pairs(axis, offset):
    return [(index, index ^ offset) for index in range(lax.axis_size(axis))]


def swap(value, axis, offset):
    return lax.ppermute(value, axis, partner_pairs(axis, offset))


MIB = 1024 * 1024
ADAM_PARAMS = pltpu.CompilerParams(vmem_limit_bytes=32 * MIB)


def attention_params(length):
    return pltpu.CompilerParams(vmem_limit_bytes=min(56, length * length // 8192) * MIB)


def adam_values(weight, first, second, grads, rate, decay):
    first_new = BETA_ONE * first + (1.0 - BETA_ONE) * grads
    second_new = BETA_TWO * second + (1.0 - BETA_TWO) * grads * grads
    first_hat = first_new * (1.0 / (1.0 - BETA_ONE**STEP))
    root = jnp.sqrt(second_new * (1.0 / (1.0 - BETA_TWO**STEP)))
    weight_new = weight - rate * (first_hat / (root + EPS_ADAM) + decay * weight)
    return (weight_new, first_new, second_new)


def in_columns(grads):
    seq_size, slots, rows, part = grads.shape
    return wide(grads).transpose(2, 1, 0, 3).reshape(rows, slots, seq_size * part)


def update_attention(weight, first, second, grads):
    seq_size, slots, rows, part = grads.shape
    width = seq_size * part
    if part % 128:
        new = adam_update(weight, first, second, in_columns(grads), attention_rates(), DECAY)
        return new[0], new[1], new[2][:, :3], new[2][:, 3]
    chunk = 2
    scales = [D ** (-0.5), (32 * D) ** (-0.5), D ** (-0.5), (HEADS * HEAD_DIM // 64) ** (-0.5)]

    def body(w_ref, m_ref, v_ref, g_ref, w_out, m_out, v_out, o_out):
        for slot in range(slots):
            for item in range(chunk):
                cols = slice(item * part, (item + 1) * part)
                new = adam_values(
                    w_ref[:, slot, cols],
                    m_ref[:, slot, cols],
                    v_ref[:, slot, cols],
                    wide(g_ref[item, slot]),
                    3.0 * scales[slot],
                    DECAY,
                )
                w_out[:, slot, cols] = new[0]
                m_out[:, slot, cols] = new[1]
                if slot < slots - 1:
                    v_out[slot, :, cols] = new[2]
                else:
                    o_out[:, cols] = new[2]

    state_spec = pl.BlockSpec((rows, slots, chunk * part), lambda j: (0, 0, j))
    new = pl.pallas_call(
        body,
        grid=(seq_size // chunk,),
        in_specs=[state_spec] * 3
        + [pl.BlockSpec((chunk, slots, rows, part), lambda j: (j, 0, 0, 0))],
        out_specs=[
            state_spec,
            state_spec,
            pl.BlockSpec((slots - 1, rows, chunk * part), lambda j: (0, 0, j)),
            pl.BlockSpec((rows, chunk * part), lambda j: (0, j)),
        ],
        out_shape=[
            jax.ShapeDtypeStruct(weight.shape, jnp.float32),
            jax.ShapeDtypeStruct(weight.shape, jnp.float32),
            jax.ShapeDtypeStruct((slots - 1, rows, width), jnp.float32),
            jax.ShapeDtypeStruct((rows, width), jnp.float32),
        ],
        compiler_params=ADAM_PARAMS,
        cost_estimate=pl.CostEstimate(
            flops=20 * weight.size, bytes_accessed=26 * weight.size, transcendentals=weight.size
        ),
    )(weight, first, second, grads)
    return new[0], new[1], new[2].transpose(1, 0, 2), new[3]


def update_feed(weight, first, second, grads):
    seq_size, slots, rows, part = grads.shape
    if part % 128:
        return adam_update(weight, first, second, in_columns(grads), feed_rates(), DECAY)

    def body(w_ref, m_ref, v_ref, g_ref, w_out, m_out, v_out):
        rate = jnp.where(pl.program_id(0) == slots - 1, 3.0 * FF ** (-0.5), 3.0 * D ** (-0.5))
        for item in range(chunk):
            cols = slice(item * part, (item + 1) * part)
            new = adam_values(
                w_ref[0, :, cols],
                m_ref[0, :, cols],
                v_ref[0, :, cols],
                wide(g_ref[item, 0]),
                rate,
                DECAY,
            )
            for ref, value in zip((w_out, m_out, v_out), new):
                ref[0, :, cols] = value

    chunk = 4
    state_spec = pl.BlockSpec((1, rows, chunk * part), lambda slot, j: (slot, 0, j))
    state = [item.transpose(1, 0, 2) for item in (weight, first, second)]
    new = pl.pallas_call(
        body,
        grid=(slots, seq_size // chunk),
        in_specs=[state_spec] * 3
        + [pl.BlockSpec((chunk, 1, rows, part), lambda slot, j: (j, slot, 0, 0))],
        out_specs=[state_spec] * 3,
        out_shape=[jax.ShapeDtypeStruct(state[0].shape, jnp.float32)] * 3,
        compiler_params=ADAM_PARAMS,
        cost_estimate=pl.CostEstimate(
            flops=20 * weight.size, bytes_accessed=26 * weight.size, transcendentals=weight.size
        ),
    )(*state, grads)
    return [item.transpose(1, 0, 2) for item in new]


def head_probs(query, key, bias, same_doc):
    scores = lax.dot_general(
        query, key, (((1,), (1,)), ((), ())), preferred_element_type=jnp.float32
    )
    scores = jnp.where(same_doc, scores + bias, NEG_BIG)
    exp_scores = jnp.exp(scores - jnp.max(scores, axis=-1, keepdims=True))
    return exp_scores * (1.0 / jnp.sum(exp_scores, axis=-1, keepdims=True))


def attention_specs(seq_size, rows):
    length = seq_size * rows
    tokens_spec = pl.BlockSpec((seq_size, 1, rows, 128), lambda pair, m: (0, m, 0, pair))
    return tokens_spec, [
        pl.BlockSpec((2, length, length), lambda pair, m: (pair, 0, 0)),
        pl.BlockSpec((1, length, 1), lambda pair, m: (m, 0, 0)),
        pl.BlockSpec((1, 1, length), lambda pair, m: (m, 0, 0)),
    ]


def attention_forward(query, key, value, bias, segments):
    seq_size, micro_count, rows, part = query.shape
    length = seq_size * rows
    tokens_spec, other_specs = attention_specs(seq_size, rows)

    def body(q_ref, k_ref, v_ref, bias_ref, seg_q_ref, seg_k_ref, out_ref):
        q, k, v = [ref[:, 0].reshape(length, 128) for ref in (q_ref, k_ref, v_ref)]
        same_doc = seg_q_ref[0] == seg_k_ref[0]
        outs = []
        for h in range(2):
            cols = slice(h * HEAD_DIM, (h + 1) * HEAD_DIM)
            probs = head_probs(q[:, cols], k[:, cols], bias_ref[h], same_doc)
            outs.append(dot(probs.astype(jnp.bfloat16), v[:, cols]))
        out = jnp.concatenate(outs, 1).astype(jnp.bfloat16)
        out_ref[...] = out.reshape(seq_size, 1, rows, 128)

    return pl.pallas_call(
        body,
        grid=(part // 128, micro_count),
        in_specs=[tokens_spec] * 3 + other_specs,
        out_specs=tokens_spec,
        out_shape=jax.ShapeDtypeStruct(query.shape, jnp.bfloat16),
        compiler_params=attention_params(length),
        cost_estimate=pl.CostEstimate(
            flops=6000 * length * query.size // HEAD_DIM,
            bytes_accessed=8 * query.size + bias.size * 4,
            transcendentals=length * query.size // HEAD_DIM,
        ),
    )(query, key, value, bias, segments[:, :, None], segments[:, None, :])


def attention_backward(query, key, value, grad_out, bias, segments):
    seq_size, micro_count, rows, part = query.shape
    length = seq_size * rows
    tokens_spec, other_specs = attention_specs(seq_size, rows)

    def body(
        q_ref, k_ref, v_ref, g_ref, bias_ref, seg_q_ref, seg_k_ref, dq_ref, dk_ref, dv_ref, ds_ref
    ):
        q, k, v, g = [ref[:, 0].reshape(length, 128) for ref in (q_ref, k_ref, v_ref, g_ref)]
        same_doc = seg_q_ref[0] == seg_k_ref[0]
        first = pl.program_id(1) == 0
        grads = ([], [], [])
        for h in range(2):
            cols = slice(h * HEAD_DIM, (h + 1) * HEAD_DIM)
            probs = head_probs(q[:, cols], k[:, cols], bias_ref[h], same_doc)
            grad_probs = dot_t(g[:, cols], v[:, cols])
            row_dot = jnp.sum(probs * grad_probs, axis=-1, keepdims=True)
            grad_scores = (probs * (grad_probs - row_dot)).astype(jnp.bfloat16)
            wide = grad_scores.astype(jnp.float32)
            ds_ref[h] = jnp.where(first, wide, ds_ref[h] + wide)
            grads[0].append(dot(grad_scores, k[:, cols]))
            grads[1].append(outer_sum(grad_scores, q[:, cols]))
            grads[2].append(outer_sum(probs.astype(jnp.bfloat16), g[:, cols]))
        for ref, parts in zip((dq_ref, dk_ref, dv_ref), grads):
            joined = jnp.concatenate(parts, 1).astype(jnp.bfloat16)
            ref[...] = joined.reshape(seq_size, 1, rows, 128)

    return pl.pallas_call(
        body,
        grid=(part // 128, micro_count),
        in_specs=[tokens_spec] * 4 + other_specs,
        out_specs=[tokens_spec] * 3
        + [pl.BlockSpec((2, length, length), lambda pair, m: (pair, 0, 0))],
        out_shape=[jax.ShapeDtypeStruct(query.shape, jnp.bfloat16)] * 3
        + [jax.ShapeDtypeStruct((part // HEAD_DIM, length, length), jnp.float32)],
        compiler_params=attention_params(length),
        cost_estimate=pl.CostEstimate(
            flops=8000 * length * query.size // HEAD_DIM,
            bytes_accessed=14 * query.size + bias.size * 8,
            transcendentals=length * query.size // HEAD_DIM,
        ),
    )(query, key, value, grad_out, bias, segments[:, :, None], segments[:, None, :])


def gather_dp_first(mine):
    if lax.axis_size("dp") != 4:
        return [lax.all_gather(mine, "dp", axis=2)]
    return [mine, swap(mine, "dp", 1), swap(mine, "dp", 2)]


def gather_dp_second(items):
    if len(items) == 1:
        full = items[0]
    else:
        mine, one, two = items
        me = lax.axis_index("dp")
        half = mine.shape[1] // 2
        low = swap(one[:, :half], "dp", 2)
        high = swap(two[:, half:], "dp", 1)
        full = jnp.zeros(mine.shape[:2] + (4,) + mine.shape[2:], mine.dtype)
        for piece, source, start in (
            (mine, 0, 0),
            (one, 1, 0),
            (two, 2, 0),
            (low, 3, 0),
            (high, 3, half),
        ):
            full = lax.dynamic_update_slice(full, piece[:, :, None], (0, start, me ^ source, 0, 0))
    return full.reshape(full.shape[0], -1, full.shape[-1])


def wide(value):
    return value.astype(jnp.float32)


def scatter_dp_first(partial):
    if lax.axis_size("dp") != 4:
        return [lax.psum_scatter(partial, "dp", scatter_dimension=2)]
    me = lax.axis_index("dp")
    half = partial.shape[1] // 2
    pieces = [lax.dynamic_index_in_dim(partial, me ^ k, 2, keepdims=False) for k in range(4)]
    low = [piece[:, :half] for piece in pieces]
    high = [piece[:, half:] for piece in pieces]
    return low[:3] + high[:3] + [swap(low[3], "dp", 1), swap(high[3], "dp", 2)]


def scatter_dp_second(items):
    if len(items) == 1:
        return items
    low = items[:3]
    high = items[3:6]
    low_two = (wide(low[2]) + wide(items[6])).astype(jnp.bfloat16)
    high_one = (wide(high[1]) + wide(items[7])).astype(jnp.bfloat16)
    return [low[0], high[0], swap(low[1], "dp", 1), swap(high[2], "dp", 2), low_two, high_one]


def scatter_dp_third(items):
    if len(items) == 1:
        return items[0]
    low, high, low_more, high_more, low_two, high_one = items
    low_sum = wide(low) + wide(low_more) + wide(swap(low_two, "dp", 2))
    high_sum = wide(high) + wide(high_more) + wide(swap(high_one, "dp", 1))
    return jnp.concatenate([low_sum, high_sum], 1).astype(jnp.bfloat16)


def to_columns(weight):
    seq_size = lax.axis_size("seq")
    slots, rows, width = weight.shape
    send = weight.reshape(slots, rows, seq_size, width // seq_size).transpose(2, 0, 1, 3)
    return lax.all_to_all(send, "seq", 0, 0).transpose(1, 0, 2, 3)


def to_rows(mine):
    return lax.all_to_all(mine.transpose(1, 0, 2, 3), "seq", 0, 0)


def after(value, *earlier):
    return lax.optimization_barrier((value,) + earlier)[0]


def to_rows_first(grads):
    seq_size = lax.axis_size("seq")
    dp_size = lax.axis_size("dp")
    partial = jnp.stack([grad.astype(jnp.bfloat16) for grad in grads], 0)
    slots, total, part = partial.shape
    rows = total // (seq_size * dp_size)
    return scatter_dp_first(partial.reshape(slots, seq_size, dp_size, rows, part))


def sum_all(value):
    for axis in ("seq", "dp"):
        offset = 1
        while offset < lax.axis_size(axis):
            value = value + swap(value, axis, offset)
            offset = offset * 2
    return value


def gather_tokens(local_rows):
    full = lax.all_gather(local_rows, "seq", axis=0)
    return full.reshape(-1, local_rows.shape[-1])


def scatter_tokens(partial, shape):
    send = partial.astype(jnp.bfloat16).reshape((lax.axis_size("seq"),) + shape)
    return lax.psum_scatter(send, "seq", scatter_dimension=0).astype(jnp.float32)


def local(
    tokens,
    segments,
    cotangent,
    attention_weight,
    attention_first,
    attention_second,
    feed_weight,
    feed_first,
    feed_second,
    gains,
    gains_first,
    gains_second,
    rel_table,
    table_first,
    table_second,
):
    micro_count, local_rows, width = tokens.shape
    shape = tokens.shape
    seq_size = lax.axis_size("seq")
    seq_len = local_rows * seq_size
    heads_here = HEADS // seq_size
    part = heads_here * HEAD_DIM
    seq_index = lax.axis_index("seq")

    positions = jnp.arange(seq_len, dtype=jnp.int32)
    buckets = rel_bucket(positions[None, :] - positions[:, None])
    bucket_match = buckets[None, :, :] == jnp.arange(NUM_BUCKETS, dtype=jnp.int32)[:, None, None]
    table_here = lax.dynamic_slice_in_dim(rel_table, seq_index * heads_here, heads_here, 1)
    bias = jnp.einsum(
        "atj,ao->otj",
        bucket_match.astype(jnp.float32),
        table_here,
        precision=HIGHEST,
        preferred_element_type=jnp.float32,
    )
    attention_slots = attention_weight.transpose(1, 0, 2).astype(jnp.bfloat16)
    feed_slots = feed_weight.transpose(1, 0, 2).astype(jnp.bfloat16)
    inputs = tokens.astype(jnp.float32)
    normed_here = rms_norm(inputs, gains[0]).astype(jnp.bfloat16)
    attention_mine, normed_here, bias, feed_slots = lax.optimization_barrier(
        (to_columns(attention_slots), normed_here, bias, feed_slots)
    )
    normed_one = gather_tokens(normed_here)
    attention_items, late_cotangent = lax.optimization_barrier(
        (gather_dp_first(attention_mine), cotangent)
    )
    attention_low = gather_dp_second(attention_items)
    weight_out = attention_low[3]

    def as_blocks(matrix):
        return matrix.astype(jnp.bfloat16).reshape(seq_size, micro_count, local_rows, part)

    grad_out = gather_tokens(late_cotangent)
    normed_one, feed_slots = lax.optimization_barrier((normed_one, feed_slots))
    query, key, value = [
        as_blocks(dot(normed_one, attention_low[slot])) for slot in range(3)
    ]
    feed_mine = to_columns(feed_slots)
    attended = attention_forward(query, key, value, bias, segments).reshape(-1, part)
    attention_partial, grad_out, feed_mine = lax.optimization_barrier(
        (dot_t(attended, weight_out).astype(jnp.bfloat16), grad_out, feed_mine)
    )
    feed_gathered = gather_dp_first(feed_mine)
    attention_out = scatter_tokens(attention_partial, shape)
    attention_out, feed_gathered = lax.optimization_barrier((attention_out, feed_gathered))
    feed_low = gather_dp_second(feed_gathered)
    weight_gate, weight_up, weight_down = feed_low[0], feed_low[1], feed_low[2]
    hidden_state = inputs + attention_out
    normed_two = gather_tokens(rms_norm(hidden_state, gains[1]).astype(jnp.bfloat16))
    grad_inner = dot(grad_out, weight_down)
    inner, grad_gate, grad_up, grad_two = feed_middle(
        normed_two, grad_inner, weight_gate, weight_up
    )
    feed_partial = dot_t(inner, weight_down).astype(jnp.bfloat16)
    grad_normed_two = scatter_tokens(grad_two, shape)
    grads_feed = [
        outer_sum(normed_two, grad_gate).astype(jnp.bfloat16),
        outer_sum(normed_two, grad_up).astype(jnp.bfloat16),
        outer_sum(grad_out, inner).astype(jnp.bfloat16),
    ]
    feed_steps = to_rows_first(grads_feed)
    grad_normed_two, feed_steps, feed_partial = lax.optimization_barrier(
        (grad_normed_two, feed_steps, feed_partial)
    )
    feed_steps = scatter_dp_second(feed_steps)
    grad_hidden_norm, grad_gain_two = norm_back(hidden_state, gains[1], grad_normed_two)
    grad_hidden = cotangent.astype(jnp.float32) + grad_hidden_norm
    grad_branch = gather_tokens(grad_hidden.astype(jnp.bfloat16))
    grad_branch, feed_mine_grad = lax.optimization_barrier(
        (grad_branch, scatter_dp_third(feed_steps))
    )
    grad_attended = as_blocks(dot(grad_branch, weight_out))
    feed_total = to_rows(feed_mine_grad)
    grad_query, grad_key, grad_value, score_sums = attention_backward(
        query, key, value, grad_attended, bias, segments
    )
    grad_table_here = jnp.einsum(
        "hij,zij->zh",
        score_sums.astype(jnp.bfloat16),
        bucket_match.astype(jnp.bfloat16),
        preferred_element_type=jnp.float32,
    )
    grad_qkv = [item.reshape(-1, part) for item in (grad_query, grad_key, grad_value)]
    normed_partial = sum(dot_t(grad_qkv[slot], attention_low[slot]) for slot in range(3))
    normed_partial, feed_total = lax.optimization_barrier(
        (normed_partial.astype(jnp.bfloat16), feed_total)
    )
    grad_normed_one = scatter_tokens(normed_partial, shape)
    block_rows = hidden_state + scatter_tokens(after(feed_partial, grad_normed_one), shape)
    block_rows = block_rows.astype(jnp.bfloat16)
    attention_steps = to_rows_first(
        [outer_sum(normed_one, item) for item in grad_qkv] + [outer_sum(grad_branch, attended)]
    )
    attention_total = to_rows(scatter_dp_third(scatter_dp_second(attention_steps)))
    grad_input_norm, grad_gain_one = norm_back(inputs, gains[0], grad_normed_one)
    grad_rows = (grad_hidden + grad_input_norm).astype(jnp.bfloat16)
    grad_table = lax.dynamic_update_slice_in_dim(
        jnp.zeros((NUM_BUCKETS, HEADS), jnp.float32), grad_table_here, seq_index * heads_here, 1
    )
    new_feed = update_feed(feed_weight, feed_first, feed_second, feed_total)
    small = jnp.concatenate([grad_gain_one, grad_gain_two, grad_table.reshape(-1)])
    small, new_feed = lax.optimization_barrier((small, new_feed))
    small = sum_all(small.reshape(-1, 128)).reshape(-1)
    gains_total = small[: 2 * width].reshape(2, width)
    table_total = small[2 * width :].reshape(NUM_BUCKETS, HEADS)
    new_attention = update_attention(
        attention_weight, attention_first, attention_second, attention_total
    )
    new_gains = adam_update(gains, gains_first, gains_second, gains_total, 0.6, 0.0)
    new_table = adam_update(rel_table, table_first, table_second, table_total, 1.5, 0.0)
    return (
        block_rows,
        grad_rows,
        new_attention[0],
        new_attention[1],
        new_attention[2],
        new_attention[3],
        new_feed[0],
        new_feed[1],
        new_feed[2],
        new_gains[0],
        new_gains[1],
        new_gains[2],
        new_table[0],
        new_table[1],
        new_table[2],
    )


def solution(mesh):
    in_specs = (
        P("dp", "seq", None),
        P("dp", None),
        P("dp", "seq", None),
        P(("seq", "dp"), None, None),
        P(("seq", "dp"), None, None),
        P(("seq", "dp"), None, None),
        P(("seq", "dp"), None, None),
        P(("seq", "dp"), None, None),
        P(("seq", "dp"), None, None),
        P(),
        P(),
        P(),
        P(),
        P(),
        P(),
    )
    out_specs = (
        P("dp", "seq", None),
        P("dp", "seq", None),
        P(("seq", "dp"), None, None),
        P(("seq", "dp"), None, None),
        P(("seq", "dp"), None, None),
        P(("seq", "dp"), None),
        P(("seq", "dp"), None, None),
        P(("seq", "dp"), None, None),
        P(("seq", "dp"), None, None),
        P(),
        P(),
        P(),
        P(),
        P(),
        P(),
    )
    return jax.shard_map(local, mesh=mesh, in_specs=in_specs, out_specs=out_specs, check_vma=False)
```

```python
import math

import jax
import jax.numpy as jnp
from jax import lax
from jax.experimental import pallas as pl
from jax.experimental.pallas import tpu as pltpu
from jax.sharding import PartitionSpec as P

D = 2048
HEADS = 32
HEAD_DIM = 64
FF = 5120
NUM_BUCKETS = 32
MAX_DIST = 128
STEP = 10


NORM_EPSILON = 1e-06
NEG_BIG = -1000000000.0
BETA_ONE = 0.9
BETA_TWO = 0.95
EPS_ADAM = 1e-08
DECAY = 0.1
HIGHEST = lax.Precision.HIGHEST


def rms_norm(values, gain_vec):
    inv_root = lax.rsqrt(jnp.mean(values * values, axis=-1, keepdims=True) + NORM_EPSILON)
    return values * inv_root * gain_vec


def bucket_edges():
    half_count = NUM_BUCKETS // 2
    exact_count = half_count // 2
    log_count = half_count - exact_count
    far_ratio = MAX_DIST // exact_count
    edge_list = []
    for step_index in range(1, log_count):
        edge_at = exact_count
        while edge_at**log_count < exact_count**log_count * far_ratio**step_index:
            edge_at = edge_at + 1
        edge_list.append(edge_at)
    return edge_list


def rel_bucket(relative):
    half_count = NUM_BUCKETS // 2
    exact_count = half_count // 2
    distance = jnp.abs(relative)
    far_bucket = jnp.full(relative.shape, exact_count, jnp.int32)
    for edge_at in bucket_edges():
        far_bucket = far_bucket + (distance >= edge_at).astype(jnp.int32)
    near_far = jnp.where(distance < exact_count, distance, far_bucket)
    return near_far + jnp.where(relative > 0, half_count, 0)


def adam_update(weight, first, second, grads, rate, decay):
    first_new = BETA_ONE * first + (1.0 - BETA_ONE) * grads
    second_new = BETA_TWO * second + (1.0 - BETA_TWO) * grads * grads
    first_hat = first_new / (1.0 - BETA_ONE**STEP)
    second_hat = second_new / (1.0 - BETA_TWO**STEP)
    weight_new = weight - rate * (first_hat / (jnp.sqrt(second_hat) + EPS_ADAM) + decay * weight)
    return (weight_new, first_new, second_new)


def attention_rates():
    return 3.0 * jnp.array(
        [D ** (-0.5), (32 * D) ** (-0.5), D ** (-0.5), (HEADS * HEAD_DIM // 64) ** (-0.5)],
        jnp.float32,
    ).reshape(1, 4, 1)


def feed_rates():
    return 3.0 * jnp.array([D ** (-0.5), D ** (-0.5), FF ** (-0.5)], jnp.float32).reshape(1, 3, 1)


def dot(left, right):
    return jnp.dot(left, right, preferred_element_type=jnp.float32)


def dot_t(left, right):
    return lax.dot_general(
        left, right, (((1,), (1,)), ((), ())), preferred_element_type=jnp.float32
    )


def outer_sum(left, right):
    return lax.dot_general(
        left, right, (((0,), (0,)), ((), ())), preferred_element_type=jnp.float32
    )


def norm_stats(values):
    return lax.rsqrt(jnp.mean(values * values, axis=-1, keepdims=True) + NORM_EPSILON)


def norm_back(values, gain_vec, grads):
    inv_root = norm_stats(values)
    unit = values * inv_root
    scaled = grads * gain_vec
    grad_in = inv_root * (scaled - unit * jnp.mean(unit * scaled, axis=-1, keepdims=True))
    return grad_in, jnp.sum(grads * unit, axis=(0, 1))


def feed_middle(normed, grad_inner, weight_gate, weight_up):
    tokens, width = normed.shape
    hidden = weight_gate.shape[1]
    block = min(512, tokens)
    scale = (2.0 / math.pi) ** 0.5

    def body(n_ref, gi_ref, wg_ref, wu_ref, inner_ref, gg_ref, gu_ref, out_ref):
        gate = dot(n_ref[...], wg_ref[...])
        up = dot(n_ref[...], wu_ref[...])
        grad_inner = gi_ref[...]
        squared = gate * gate
        tanh = jnp.tanh(scale * (gate + 0.044715 * (squared * gate)))
        half = 0.5 * (1.0 + tanh)
        act = gate * half
        slope = half + 0.5 * gate * (1.0 - tanh * tanh) * (scale * (1.0 + 0.134145 * squared))
        inner_ref[...] = (act * up).astype(jnp.bfloat16)
        grad_gate = (grad_inner * up * slope).astype(jnp.bfloat16)
        grad_up = (grad_inner * act).astype(jnp.bfloat16)
        gg_ref[...] = grad_gate
        gu_ref[...] = grad_up
        total = dot_t(grad_gate, wg_ref[...]) + dot_t(grad_up, wu_ref[...])
        out_ref[...] = total.astype(jnp.bfloat16)

    rows = pl.BlockSpec((block, width), lambda i: (i, 0))
    units = pl.BlockSpec((block, hidden), lambda i: (i, 0))
    weights = pl.BlockSpec((width, hidden), lambda i: (0, 0))
    low_units = jax.ShapeDtypeStruct((tokens, hidden), jnp.bfloat16)
    return pl.pallas_call(
        body,
        grid=(tokens // block,),
        in_specs=[rows, units, weights, weights],
        out_specs=[units, units, units, rows],
        out_shape=[
            low_units,
            low_units,
            low_units,
            jax.ShapeDtypeStruct((tokens, width), jnp.bfloat16),
        ],
        compiler_params=pltpu.CompilerParams(vmem_limit_bytes=56 * MIB),
        cost_estimate=pl.CostEstimate(
            flops=8 * tokens * width * hidden,
            bytes_accessed=4 * tokens * width + 10 * tokens * hidden + 4 * width * hidden,
            transcendentals=tokens * hidden,
        ),
    )(normed, grad_inner, weight_gate, weight_up)


def partner_pairs(axis, offset):
    return [(index, index ^ offset) for index in range(lax.axis_size(axis))]


def swap(value, axis, offset):
    return lax.ppermute(value, axis, partner_pairs(axis, offset))


MIB = 1024 * 1024
ADAM_PARAMS = pltpu.CompilerParams(vmem_limit_bytes=56 * MIB)


def attention_params(length):
    return pltpu.CompilerParams(vmem_limit_bytes=56 * MIB)


def adam_values(weight, first, second, grads, rate, decay):
    first_new = BETA_ONE * first + (1.0 - BETA_ONE) * grads
    second_new = BETA_TWO * second + (1.0 - BETA_TWO) * grads * grads
    first_hat = first_new * (1.0 / (1.0 - BETA_ONE**STEP))
    root = jnp.sqrt(second_new * (1.0 / (1.0 - BETA_TWO**STEP)))
    weight_new = weight - rate * (first_hat / (root + EPS_ADAM) + decay * weight)
    return (weight_new, first_new, second_new)


def in_columns(grads):
    seq_size, slots, rows, part = grads.shape
    return wide(grads).transpose(2, 1, 0, 3).reshape(rows, slots, seq_size * part)


def update_attention(weight, first, second, grads):
    seq_size, slots, rows, part = grads.shape
    width = seq_size * part
    if part % 128:
        new = adam_update(weight, first, second, in_columns(grads), attention_rates(), DECAY)
        return new[0], new[1], new[2][:, :3], new[2][:, 3]
    chunk = 2
    scales = [D ** (-0.5), (32 * D) ** (-0.5), D ** (-0.5), (HEADS * HEAD_DIM // 64) ** (-0.5)]

    def body(w_ref, m_ref, v_ref, g_ref, w_out, m_out, v_out, o_out):
        for slot in range(slots):
            for item in range(chunk):
                cols = slice(item * part, (item + 1) * part)
                new = adam_values(
                    w_ref[:, slot, cols],
                    m_ref[:, slot, cols],
                    v_ref[:, slot, cols],
                    wide(g_ref[item, slot]),
                    3.0 * scales[slot],
                    DECAY,
                )
                w_out[:, slot, cols] = new[0]
                m_out[:, slot, cols] = new[1]
                if slot < slots - 1:
                    v_out[slot, :, cols] = new[2]
                else:
                    o_out[:, cols] = new[2]

    state_spec = pl.BlockSpec((rows, slots, chunk * part), lambda j: (0, 0, j))
    new = pl.pallas_call(
        body,
        grid=(seq_size // chunk,),
        in_specs=[state_spec] * 3
        + [pl.BlockSpec((chunk, slots, rows, part), lambda j: (j, 0, 0, 0))],
        out_specs=[
            state_spec,
            state_spec,
            pl.BlockSpec((slots - 1, rows, chunk * part), lambda j: (0, 0, j)),
            pl.BlockSpec((rows, chunk * part), lambda j: (0, j)),
        ],
        out_shape=[
            jax.ShapeDtypeStruct(weight.shape, jnp.float32),
            jax.ShapeDtypeStruct(weight.shape, jnp.float32),
            jax.ShapeDtypeStruct((slots - 1, rows, width), jnp.float32),
            jax.ShapeDtypeStruct((rows, width), jnp.float32),
        ],
        compiler_params=ADAM_PARAMS,
        cost_estimate=pl.CostEstimate(
            flops=20 * weight.size, bytes_accessed=26 * weight.size, transcendentals=weight.size
        ),
    )(weight, first, second, grads)
    return new[0], new[1], new[2].transpose(1, 0, 2), new[3]


def update_feed(weight, first, second, grads):
    seq_size, slots, rows, part = grads.shape
    if part % 128:
        return adam_update(weight, first, second, in_columns(grads), feed_rates(), DECAY)

    def body(w_ref, m_ref, v_ref, g_ref, w_out, m_out, v_out):
        rate = jnp.where(pl.program_id(0) == slots - 1, 3.0 * FF ** (-0.5), 3.0 * D ** (-0.5))
        for item in range(chunk):
            cols = slice(item * part, (item + 1) * part)
            new = adam_values(
                w_ref[0, :, cols],
                m_ref[0, :, cols],
                v_ref[0, :, cols],
                wide(g_ref[item, 0]),
                rate,
                DECAY,
            )
            for ref, value in zip((w_out, m_out, v_out), new):
                ref[0, :, cols] = value

    chunk = 4
    state_spec = pl.BlockSpec((1, rows, chunk * part), lambda slot, j: (slot, 0, j))
    state = [item.transpose(1, 0, 2) for item in (weight, first, second)]
    new = pl.pallas_call(
        body,
        grid=(slots, seq_size // chunk),
        in_specs=[state_spec] * 3
        + [pl.BlockSpec((chunk, 1, rows, part), lambda slot, j: (j, slot, 0, 0))],
        out_specs=[state_spec] * 3,
        out_shape=[jax.ShapeDtypeStruct(state[0].shape, jnp.float32)] * 3,
        compiler_params=ADAM_PARAMS,
        cost_estimate=pl.CostEstimate(
            flops=20 * weight.size, bytes_accessed=26 * weight.size, transcendentals=weight.size
        ),
    )(*state, grads)
    return [item.transpose(1, 0, 2) for item in new]


def head_probs(query, key, bias, same_doc):
    scores = lax.dot_general(
        query, key, (((1,), (1,)), ((), ())), preferred_element_type=jnp.float32
    )
    scores = jnp.where(same_doc, scores + bias, NEG_BIG)
    exp_scores = jnp.exp(scores - jnp.max(scores, axis=-1, keepdims=True))
    return exp_scores * (1.0 / jnp.sum(exp_scores, axis=-1, keepdims=True))


def attention_specs(seq_size, rows):
    length = seq_size * rows
    tokens_spec = pl.BlockSpec((seq_size, 1, rows, 128), lambda pair, m: (0, m, 0, pair))
    return tokens_spec, [
        pl.BlockSpec((2, length, length), lambda pair, m: (pair, 0, 0)),
        pl.BlockSpec((1, length, 1), lambda pair, m: (m, 0, 0)),
        pl.BlockSpec((1, 1, length), lambda pair, m: (m, 0, 0)),
    ]


def attention_forward(query, key, value, bias, segments):
    seq_size, micro_count, rows, part = query.shape
    length = seq_size * rows
    tokens_spec, other_specs = attention_specs(seq_size, rows)

    def body(q_ref, k_ref, v_ref, bias_ref, seg_q_ref, seg_k_ref, out_ref):
        q, k, v = [ref[:, 0].reshape(length, 128) for ref in (q_ref, k_ref, v_ref)]
        same_doc = seg_q_ref[0] == seg_k_ref[0]
        outs = []
        for h in range(2):
            cols = slice(h * HEAD_DIM, (h + 1) * HEAD_DIM)
            probs = head_probs(q[:, cols], k[:, cols], bias_ref[h], same_doc)
            outs.append(dot(probs.astype(jnp.bfloat16), v[:, cols]))
        out = jnp.concatenate(outs, 1).astype(jnp.bfloat16)
        out_ref[...] = out.reshape(seq_size, 1, rows, 128)

    return pl.pallas_call(
        body,
        grid=(part // 128, micro_count),
        in_specs=[tokens_spec] * 3 + other_specs,
        out_specs=tokens_spec,
        out_shape=jax.ShapeDtypeStruct(query.shape, jnp.bfloat16),
        compiler_params=attention_params(length),
        cost_estimate=pl.CostEstimate(
            flops=6000 * length * query.size // HEAD_DIM,
            bytes_accessed=8 * query.size + bias.size * 4,
            transcendentals=length * query.size // HEAD_DIM,
        ),
    )(query, key, value, bias, segments[:, :, None], segments[:, None, :])


def attention_backward(query, key, value, grad_out, bias, segments):
    seq_size, micro_count, rows, part = query.shape
    length = seq_size * rows
    tokens_spec, other_specs = attention_specs(seq_size, rows)

    def body(
        q_ref, k_ref, v_ref, g_ref, bias_ref, seg_q_ref, seg_k_ref, dq_ref, dk_ref, dv_ref, ds_ref
    ):
        q, k, v, g = [ref[:, 0].reshape(length, 128) for ref in (q_ref, k_ref, v_ref, g_ref)]
        same_doc = seg_q_ref[0] == seg_k_ref[0]
        first = pl.program_id(1) == 0
        grads = ([], [], [])
        for h in range(2):
            cols = slice(h * HEAD_DIM, (h + 1) * HEAD_DIM)
            probs = head_probs(q[:, cols], k[:, cols], bias_ref[h], same_doc)
            grad_probs = dot_t(g[:, cols], v[:, cols])
            row_dot = jnp.sum(probs * grad_probs, axis=-1, keepdims=True)
            grad_scores = (probs * (grad_probs - row_dot)).astype(jnp.bfloat16)
            wide = grad_scores.astype(jnp.float32)
            ds_ref[h] = jnp.where(first, wide, ds_ref[h] + wide)
            grads[0].append(dot(grad_scores, k[:, cols]))
            grads[1].append(outer_sum(grad_scores, q[:, cols]))
            grads[2].append(outer_sum(probs.astype(jnp.bfloat16), g[:, cols]))
        for ref, parts in zip((dq_ref, dk_ref, dv_ref), grads):
            joined = jnp.concatenate(parts, 1).astype(jnp.bfloat16)
            ref[...] = joined.reshape(seq_size, 1, rows, 128)

    return pl.pallas_call(
        body,
        grid=(part // 128, micro_count),
        in_specs=[tokens_spec] * 4 + other_specs,
        out_specs=[tokens_spec] * 3
        + [pl.BlockSpec((2, length, length), lambda pair, m: (pair, 0, 0))],
        out_shape=[jax.ShapeDtypeStruct(query.shape, jnp.bfloat16)] * 3
        + [jax.ShapeDtypeStruct((part // HEAD_DIM, length, length), jnp.float32)],
        compiler_params=attention_params(length),
        cost_estimate=pl.CostEstimate(
            flops=8000 * length * query.size // HEAD_DIM,
            bytes_accessed=14 * query.size + bias.size * 8,
            transcendentals=length * query.size // HEAD_DIM,
        ),
    )(query, key, value, grad_out, bias, segments[:, :, None], segments[:, None, :])


def gather_dp_first(mine):
    if lax.axis_size("dp") != 4:
        return [lax.all_gather(mine, "dp", axis=2)]
    return [mine, swap(mine, "dp", 1), swap(mine, "dp", 2)]


def gather_dp_second(items):
    if len(items) == 1:
        full = items[0]
    else:
        mine, one, two = items
        me = lax.axis_index("dp")
        half = mine.shape[1] // 2
        low = swap(one[:, :half], "dp", 2)
        high = swap(two[:, half:], "dp", 1)
        full = jnp.zeros(mine.shape[:2] + (4,) + mine.shape[2:], mine.dtype)
        for piece, source, start in (
            (mine, 0, 0),
            (one, 1, 0),
            (two, 2, 0),
            (low, 3, 0),
            (high, 3, half),
        ):
            full = lax.dynamic_update_slice(full, piece[:, :, None], (0, start, me ^ source, 0, 0))
    return full.reshape(full.shape[0], -1, full.shape[-1])


def wide(value):
    return value.astype(jnp.float32)


def scatter_dp_first(partial):
    if lax.axis_size("dp") != 4:
        return [lax.psum_scatter(partial, "dp", scatter_dimension=2)]
    me = lax.axis_index("dp")
    half = partial.shape[1] // 2
    pieces = [lax.dynamic_index_in_dim(partial, me ^ k, 2, keepdims=False) for k in range(4)]
    low = [piece[:, :half] for piece in pieces]
    high = [piece[:, half:] for piece in pieces]
    return low[:3] + high[:3] + [swap(low[3], "dp", 1), swap(high[3], "dp", 2)]


def scatter_dp_second(items):
    if len(items) == 1:
        return items
    low = items[:3]
    high = items[3:6]
    low_two = (wide(low[2]) + wide(items[6])).astype(jnp.bfloat16)
    high_one = (wide(high[1]) + wide(items[7])).astype(jnp.bfloat16)
    return [low[0], high[0], swap(low[1], "dp", 1), swap(high[2], "dp", 2), low_two, high_one]


def scatter_dp_third(items):
    if len(items) == 1:
        return items[0]
    low, high, low_more, high_more, low_two, high_one = items
    low_sum = wide(low) + wide(low_more) + wide(swap(low_two, "dp", 2))
    high_sum = wide(high) + wide(high_more) + wide(swap(high_one, "dp", 1))
    return jnp.concatenate([low_sum, high_sum], 1).astype(jnp.bfloat16)


def to_columns(weight):
    seq_size = lax.axis_size("seq")
    slots, rows, width = weight.shape
    send = weight.reshape(slots, rows, seq_size, width // seq_size).transpose(2, 0, 1, 3)
    return lax.all_to_all(send, "seq", 0, 0).transpose(1, 0, 2, 3)


def to_rows(mine):
    return lax.all_to_all(mine.transpose(1, 0, 2, 3), "seq", 0, 0)


def after(value, *earlier):
    return lax.optimization_barrier((value,) + earlier)[0]


def to_rows_first(grads):
    seq_size = lax.axis_size("seq")
    dp_size = lax.axis_size("dp")
    partial = jnp.stack([grad.astype(jnp.bfloat16) for grad in grads], 0)
    slots, total, part = partial.shape
    rows = total // (seq_size * dp_size)
    return scatter_dp_first(partial.reshape(slots, seq_size, dp_size, rows, part))


def sum_all(value):
    for axis in ("seq", "dp"):
        offset = 1
        while offset < lax.axis_size(axis):
            value = value + swap(value, axis, offset)
            offset = offset * 2
    return value


def gather_tokens(local_rows):
    full = lax.all_gather(local_rows, "seq", axis=0)
    return full.reshape(-1, local_rows.shape[-1])


def scatter_tokens(partial, shape):
    send = partial.astype(jnp.bfloat16).reshape((lax.axis_size("seq"),) + shape)
    return lax.psum_scatter(send, "seq", scatter_dimension=0).astype(jnp.float32)


def local(
    tokens,
    segments,
    cotangent,
    attention_weight,
    attention_first,
    attention_second,
    feed_weight,
    feed_first,
    feed_second,
    gains,
    gains_first,
    gains_second,
    rel_table,
    table_first,
    table_second,
):
    micro_count, local_rows, width = tokens.shape
    shape = tokens.shape
    seq_size = lax.axis_size("seq")
    seq_len = local_rows * seq_size
    heads_here = HEADS // seq_size
    part = heads_here * HEAD_DIM
    seq_index = lax.axis_index("seq")

    attention_slots = attention_weight.transpose(1, 0, 2).astype(jnp.bfloat16)
    feed_slots = feed_weight.transpose(1, 0, 2).astype(jnp.bfloat16)
    inputs = tokens.astype(jnp.float32)
    normed_here = rms_norm(inputs, gains[0]).astype(jnp.bfloat16)
    attention_mine, normed_here = lax.optimization_barrier(
        (to_columns(attention_slots), normed_here)
    )
    normed_one = gather_tokens(normed_here)
    attention_items, late_cotangent = lax.optimization_barrier(
        (gather_dp_first(attention_mine), cotangent)
    )
    attention_low = gather_dp_second(attention_items)
    weight_out = attention_low[3]

    positions = jnp.arange(seq_len, dtype=jnp.int32)
    buckets = rel_bucket(positions[None, :] - positions[:, None])
    bucket_match = buckets[None, :, :] == jnp.arange(NUM_BUCKETS, dtype=jnp.int32)[:, None, None]
    table_here = lax.dynamic_slice_in_dim(rel_table, seq_index * heads_here, heads_here, 1)
    bias = jnp.einsum(
        "atj,ao->otj",
        bucket_match.astype(jnp.float32),
        table_here,
        precision=HIGHEST,
        preferred_element_type=jnp.float32,
    )

    def as_blocks(matrix):
        return matrix.astype(jnp.bfloat16).reshape(seq_size, micro_count, local_rows, part)

    grad_out = gather_tokens(late_cotangent)
    query, key, value = [
        as_blocks(dot(normed_one, attention_low[slot])) for slot in range(3)
    ]
    query, key, value, feed_slots = lax.optimization_barrier((query, key, value, feed_slots))
    feed_mine = to_columns(feed_slots)
    attended = attention_forward(query, key, value, bias, segments).reshape(-1, part)
    attention_partial, grad_out, feed_mine = lax.optimization_barrier(
        (dot_t(attended, weight_out).astype(jnp.bfloat16), grad_out, feed_mine)
    )
    feed_gathered = gather_dp_first(feed_mine)
    attention_out = scatter_tokens(attention_partial, shape)
    attention_out, feed_gathered = lax.optimization_barrier((attention_out, feed_gathered))
    feed_low = gather_dp_second(feed_gathered)
    weight_gate, weight_up, weight_down = feed_low[0], feed_low[1], feed_low[2]
    hidden_state = inputs + attention_out
    normed_two = gather_tokens(rms_norm(hidden_state, gains[1]).astype(jnp.bfloat16))
    grad_inner = dot(grad_out, weight_down)
    inner, grad_gate, grad_up, grad_two = feed_middle(
        normed_two, grad_inner, weight_gate, weight_up
    )
    feed_partial = dot_t(inner, weight_down).astype(jnp.bfloat16)
    grad_normed_two = scatter_tokens(grad_two, shape)
    grads_feed = [
        outer_sum(normed_two, grad_gate).astype(jnp.bfloat16),
        outer_sum(normed_two, grad_up).astype(jnp.bfloat16),
        outer_sum(grad_out, inner).astype(jnp.bfloat16),
    ]
    feed_steps = to_rows_first(grads_feed)
    grad_normed_two, feed_steps, feed_partial = lax.optimization_barrier(
        (grad_normed_two, feed_steps, feed_partial)
    )
    feed_steps = scatter_dp_second(feed_steps)
    grad_hidden_norm, grad_gain_two = norm_back(hidden_state, gains[1], grad_normed_two)
    grad_hidden = cotangent.astype(jnp.float32) + grad_hidden_norm
    grad_branch = gather_tokens(grad_hidden.astype(jnp.bfloat16))
    grad_branch, feed_mine_grad = lax.optimization_barrier(
        (grad_branch, scatter_dp_third(feed_steps))
    )
    grad_attended = as_blocks(dot(grad_branch, weight_out))
    feed_total = to_rows(feed_mine_grad)
    grad_query, grad_key, grad_value, score_sums = attention_backward(
        query, key, value, grad_attended, bias, segments
    )
    grad_table_here = jnp.einsum(
        "hij,zij->zh",
        score_sums.astype(jnp.bfloat16),
        bucket_match.astype(jnp.bfloat16),
        preferred_element_type=jnp.float32,
    )
    grad_qkv = [item.reshape(-1, part) for item in (grad_query, grad_key, grad_value)]
    normed_partial = sum(dot_t(grad_qkv[slot], attention_low[slot]) for slot in range(3))
    normed_partial, feed_total = lax.optimization_barrier(
        (normed_partial.astype(jnp.bfloat16), feed_total)
    )
    grad_normed_one = scatter_tokens(normed_partial, shape)
    block_rows = hidden_state + scatter_tokens(after(feed_partial, grad_normed_one), shape)
    block_rows = block_rows.astype(jnp.bfloat16)
    attention_steps = to_rows_first(
        [outer_sum(normed_one, item) for item in grad_qkv] + [outer_sum(grad_branch, attended)]
    )
    attention_total = to_rows(scatter_dp_third(scatter_dp_second(attention_steps)))
    grad_input_norm, grad_gain_one = norm_back(inputs, gains[0], grad_normed_one)
    grad_rows = (grad_hidden + grad_input_norm).astype(jnp.bfloat16)
    grad_table = lax.dynamic_update_slice_in_dim(
        jnp.zeros((NUM_BUCKETS, HEADS), jnp.float32), grad_table_here, seq_index * heads_here, 1
    )
    new_feed = update_feed(feed_weight, feed_first, feed_second, feed_total)
    small = jnp.concatenate([grad_gain_one, grad_gain_two, grad_table.reshape(-1)])
    small, new_feed = lax.optimization_barrier((small, new_feed))
    small = sum_all(small.reshape(-1, 128)).reshape(-1)
    gains_total = small[: 2 * width].reshape(2, width)
    table_total = small[2 * width :].reshape(NUM_BUCKETS, HEADS)
    new_attention = update_attention(
        attention_weight, attention_first, attention_second, attention_total
    )
    new_gains = adam_update(gains, gains_first, gains_second, gains_total, 0.6, 0.0)
    new_table = adam_update(rel_table, table_first, table_second, table_total, 1.5, 0.0)
    return (
        block_rows,
        grad_rows,
        new_attention[0],
        new_attention[1],
        new_attention[2],
        new_attention[3],
        new_feed[0],
        new_feed[1],
        new_feed[2],
        new_gains[0],
        new_gains[1],
        new_gains[2],
        new_table[0],
        new_table[1],
        new_table[2],
    )


def solution(mesh):
    in_specs = (
        P("dp", "seq", None),
        P("dp", None),
        P("dp", "seq", None),
        P(("seq", "dp"), None, None),
        P(("seq", "dp"), None, None),
        P(("seq", "dp"), None, None),
        P(("seq", "dp"), None, None),
        P(("seq", "dp"), None, None),
        P(("seq", "dp"), None, None),
        P(),
        P(),
        P(),
        P(),
        P(),
        P(),
    )
    out_specs = (
        P("dp", "seq", None),
        P("dp", "seq", None),
        P(("seq", "dp"), None, None),
        P(("seq", "dp"), None, None),
        P(("seq", "dp"), None, None),
        P(("seq", "dp"), None),
        P(("seq", "dp"), None, None),
        P(("seq", "dp"), None, None),
        P(("seq", "dp"), None, None),
        P(),
        P(),
        P(),
        P(),
        P(),
        P(),
    )
    return jax.shard_map(local, mesh=mesh, in_specs=in_specs, out_specs=out_specs, check_vma=False)
```
